32 devices in a mesh: row: 16 (over z, y, core), col: 2 (over x).
Axes of the slice: x: 2, y: 2, z: 4, core: 2. Of those that a mesh axis runs over, the one named last changes fastest.
Arguments:
- stem_slab: float32 [2, 256, 256, 256], P(None, 'row', None, 'col'), may hold values from -6 to 6
- factors: float32 [32, 2, 2, 256, 256], P(('row', 'col')), may hold values from -0.25 to 0.25
- branch_owner: int32 [4], replicated, may hold values from 0 to 31
- entangle_phase: float32 [4, 256, 256], replicated, may hold values from -3.140625 to 3.140625
Outputs:
- contracted: float32 [2, 256, 256, 256], P(None, 'row', None, 'col')
The draws below stay inside these ranges and needn't reach their ends.
All inputs are finite; a program needn't handle non-finite values.
Results may differ from the reference program's by a relative error of at most 0.000039.
Values sent between devices are 32-bit elements; how exact they have to be, the bound alone decides.
No kernel may reach another device: no remote copies, remote signals or barrier semaphores. Data moves between devices by JAX's collectives and lax.ppermute only.
A program may use at most 64 MiB of HBM per device.

```python
from functools import partial
import jax
import jax.numpy as jnp
from jax import lax

W = 256
STEPS = 4
NBATCH = 256
DEVICES_ALL = 32
N_ROW = 16
N_COL = 2


def plant(drawn, rng, smallest, high):
    dims = drawn.shape
    index_at = [jax.random.randint(jax.random.fold_in(rng, axis), (), 0, dims[axis]) for axis in range(len(dims))]
    drawn = drawn.at[tuple(index_at)].set(smallest)
    longest = dims.index(max(dims))
    index_at[longest] = (index_at[longest] + 1) % dims[longest]
    return drawn.at[tuple(index_at)].set(high)


def shard_levels(rng, dims, split, least, largest):
    def one(axis_at, shards_of):
        draws = jax.random.uniform(jax.random.fold_in(jax.random.fold_in(rng, 6), axis_at), (shards_of,), jnp.float32, least / len(split), largest / len(split))
        return jnp.repeat(jnp.exp(draws), dims[axis_at] // shards_of).reshape((-1,) + (1,) * (len(dims) - axis_at - 1))

    level = one(*split[0])
    for cut in split[1:]:
        level = level * one(*cut)
    return level


def gaussian(rng, shape, scale, reach, split=(), dtype=jnp.bfloat16):
    loudness = shard_levels(rng, shape, split, -0.22, 0.18) if split else 1.0
    values = jax.random.normal(rng, shape, jnp.float32) * scale * loudness
    return jnp.minimum(jnp.maximum(values, -reach), reach).astype(dtype)


def setup_inputs(seed: int = 0) -> dict:
    key_of = jax.random.split(jax.random.key(seed), 5)
    return {
        "stem_slab": gaussian(key_of[0], (2, W, W, NBATCH), 1.0, 6.0, ((1, 16), (3, 2)), jnp.float32),
        "factors": gaussian(key_of[1], (DEVICES_ALL, 2, 2, W, W), (2 * W) ** -0.5, 0.25, ((0, 32),), jnp.float32),
        "branch_owner": plant(jax.random.randint(key_of[2], (STEPS,), 0, N_ROW * N_COL), jax.random.fold_in(key_of[2], 1), 0, (N_ROW * N_COL) - 1).astype(jnp.int32),
        "entangle_phase": jnp.clip(jax.random.uniform(key_of[3], (STEPS, W, W), jnp.float32, -3.140625, 3.140625), -3.140625, 3.140625),
    }


def complex_mix(real_part, imag_part, branch_real, branch_imag, form):
    mix = partial(jnp.einsum, form, precision=lax.Precision.HIGHEST)
    return (mix(real_part, branch_real) - mix(imag_part, branch_imag),
            mix(real_part, branch_imag) + mix(imag_part, branch_real))


def build_branch(owned):
    dot_high = partial(jnp.dot, precision=lax.Precision.HIGHEST)
    left_real, left_imag = owned[0, 0], owned[0, 1]
    right_real, right_imag = owned[1, 0], owned[1, 1]
    return (dot_high(left_real, right_real) - dot_high(left_imag, right_imag),
            dot_high(left_real, right_imag) + dot_high(left_imag, right_real))


def reference(stem_slab, factors, branch_owner, entangle_phase):
    real_part, imag_part = stem_slab[0], stem_slab[1]
    for step in range(STEPS):
        owned = lax.dynamic_index_in_dim(factors, branch_owner[step].astype(jnp.int32), 0, keepdims=False)
        branch_real, branch_imag = build_branch(owned)
        if step % 2 == 0:
            real_part, imag_part = complex_mix(real_part, imag_part, branch_real, branch_imag, "akb,kl->alb")
        else:
            real_part, imag_part = complex_mix(real_part, imag_part, branch_real, branch_imag, "akb,al->lkb")
        cosine = jnp.cos(entangle_phase[step])[:, :, None]
        sine = jnp.sin(entangle_phase[step])[:, :, None]
        real_part, imag_part = (real_part * cosine - imag_part * sine,
                                real_part * sine + imag_part * cosine)
    return jnp.stack([real_part, imag_part])
```

```python
from functools import partial

import jax
import jax.numpy as jnp
from jax import lax
from jax.experimental import pallas as pl
from jax.experimental.pallas import tpu as pltpu
from jax.sharding import PartitionSpec as P

STEPS = 4
MIB = 1024 * 1024
DOT = partial(jnp.dot, precision=lax.Precision.HIGHEST)


def build_branch(owned):
    left_real, left_imag = (owned[0, 0], owned[0, 1])
    right_real, right_imag = (owned[1, 0], owned[1, 1])
    return jnp.stack(
        [
            DOT(left_real, right_real) - DOT(left_imag, right_imag),
            DOT(left_real, right_imag) + DOT(left_imag, right_real),
        ]
    )


def swap(array, axis, size, bit):
    return lax.ppermute(array, axis, [(i, i ^ bit) for i in range(size)])


def bits_of(size):
    return [1 << i for i in range(size.bit_length() - 1)]


def broadcast_branches(own, owners, rows, cols):
    row, col = lax.axis_index("row"), lax.axis_index("col")
    mine = (owners == row * cols + col).reshape(STEPS, 1, 1, 1)
    width = own.shape[-1]
    held = jnp.where(mine, own[None], 0.0).reshape(-1, width)
    row_bits = bits_of(rows)
    halved = [("row", rows, row, b) for b in row_bits[:1]]
    halved += [("col", cols, col, b) for b in bits_of(cols)]
    halved += [("row", rows, row, b) for b in row_bits[1:2]]
    for axis, size, index, bit in halved:
        half = held.shape[0] // 2
        high = (index & bit) // bit
        keep = lax.dynamic_slice_in_dim(held, high * half, half, 0)
        send = lax.dynamic_slice_in_dim(held, (1 - high) * half, half, 0)
        held = keep + swap(send, axis, size, bit)
    for bit in row_bits[2:]:
        held = held + swap(held, "row", rows, bit)
    for axis, size, index, bit in reversed(halved):
        other = swap(held, axis, size, bit)
        high = (index & bit) != 0
        held = jnp.concatenate([jnp.where(high, other, held), jnp.where(high, held, other)], 0)
    return held.reshape(STEPS, 2, width, width)


def split(value):
    high = value.astype(jnp.bfloat16)
    low = (value - high.astype(jnp.float32)).astype(jnp.bfloat16)
    return high, low


def prepare_kernel(branch_ref, even_ref, odd_ref):
    for step in range(STEPS):
        real, imag = branch_ref[step, 0], branch_ref[step, 1]
        if step % 2:
            real, imag = real.T, imag.T
        axis = 1 if step % 2 else 0
        (rh, rl), (ih, il) = split(real), split(imag)
        to_real = jnp.concatenate([rh, rh, rl, -ih, -ih, -il], axis)
        to_imag = jnp.concatenate([ih, ih, il, rh, rh, rl], axis)
        out = jnp.concatenate([to_real, to_imag], 1 - axis)
        if step % 2:
            odd_ref[step // 2] = out
        else:
            even_ref[step // 2] = out


def prepare(branches):
    width = branches.shape[-1]
    pairs = STEPS // 2
    return pl.pallas_call(
        prepare_kernel,
        out_shape=(
            jax.ShapeDtypeStruct((pairs, 6 * width, 2 * width), jnp.bfloat16),
            jax.ShapeDtypeStruct((pairs, 2 * width, 6 * width), jnp.bfloat16),
        ),
        compiler_params=pltpu.CompilerParams(vmem_limit_bytes=48 * MIB),
        name="prepare",
    )(branches)


def absorb_kernel(stem_ref, even_ref, odd_ref, cos_ref, sin_ref, out_ref):
    width = cos_ref.shape[1]
    for item in range(stem_ref.shape[1]):
        real = stem_ref[:, item, 0].reshape(width, width)
        imag = stem_ref[:, item, 1].reshape(width, width)
        for step in range(STEPS):
            (rh, rl), (ih, il) = split(real), split(imag)
            if step % 2 == 0:
                stacked = jnp.concatenate([rh, rl, rh, ih, il, ih], 1)
                both = jnp.dot(stacked, even_ref[step // 2], preferred_element_type=jnp.float32)
                real, imag = both[:, :width], both[:, width:]
            else:
                stacked = jnp.concatenate([rh, rl, rh, ih, il, ih], 0)
                both = jnp.dot(odd_ref[step // 2], stacked, preferred_element_type=jnp.float32)
                real, imag = both[:width], both[width:]
            cosine, sine = cos_ref[step], sin_ref[step]
            real, imag = real * cosine - imag * sine, real * sine + imag * cosine
        shape = (stem_ref.shape[0], stem_ref.shape[3], width)
        out_ref[:, item, 0] = real.reshape(shape)
        out_ref[:, item, 1] = imag.reshape(shape)


def absorb(stem, even, odd, cosine, sine):
    peers, items, _, block, width = stem.shape
    per = 2 if items % 2 == 0 else 1
    spec = pl.BlockSpec((peers, per, 2, block, width), lambda i: (0, i, 0, 0, 0))
    whole = pl.BlockSpec(memory_space=pltpu.VMEM)
    flops = items * STEPS * 12 * 2 * width**3
    return pl.pallas_call(
        absorb_kernel,
        grid=(items // per,),
        in_specs=[spec, whole, whole, whole, whole],
        out_specs=spec,
        out_shape=jax.ShapeDtypeStruct(stem.shape, jnp.float32),
        cost_estimate=pl.CostEstimate(flops=flops, bytes_accessed=8 * stem.size, transcendentals=0),
        compiler_params=pltpu.CompilerParams(vmem_limit_bytes=56 * MIB),
        name="absorb",
    )(stem, even, odd, cosine, sine)


def batch_first_kernel(stem_ref, out_ref):
    for i in range(stem_ref.shape[1]):
        out_ref[:, 0, i, :] = stem_ref[0, i].T


def batch_first(stem):
    parts, rows, width, batch = stem.shape
    return pl.pallas_call(
        batch_first_kernel,
        grid=(parts, rows // 8),
        in_specs=[pl.BlockSpec((1, 8, width, batch), lambda p, r: (p, r, 0, 0))],
        out_specs=pl.BlockSpec((batch, 1, 8, width), lambda p, r: (0, p, r, 0)),
        out_shape=jax.ShapeDtypeStruct((batch, parts, rows, width), jnp.float32),
        compiler_params=pltpu.CompilerParams(vmem_limit_bytes=48 * MIB),
        name="batch_first",
    )(stem)


def batch_last_kernel(stem_ref, out_ref):
    for i in range(out_ref.shape[1]):
        out_ref[0, i] = stem_ref[:, 0, i, :].T


def batch_last(stem):
    batch, parts, rows, width = stem.shape
    return pl.pallas_call(
        batch_last_kernel,
        grid=(parts, rows // 8),
        in_specs=[pl.BlockSpec((batch, 1, 8, width), lambda p, r: (0, p, r, 0))],
        out_specs=pl.BlockSpec((1, 8, width, batch), lambda p, r: (p, r, 0, 0)),
        out_shape=jax.ShapeDtypeStruct((parts, rows, width, batch), jnp.float32),
        compiler_params=pltpu.CompilerParams(vmem_limit_bytes=48 * MIB),
        name="batch_last",
    )(stem)


def on_device(stem_slab, factors, branch_owner, entangle_phase, *, rows, cols):
    parts, block, width, batch = stem_slab.shape
    items = batch // rows
    sent = batch_first(stem_slab).reshape(rows, items, parts, block, width)
    stem = lax.all_to_all(sent, "row", 0, 0, tiled=True)
    branches = broadcast_branches(build_branch(factors[0]), branch_owner, rows, cols)
    even, odd = prepare(branches)
    stem = absorb(stem, even, odd, jnp.cos(entangle_phase), jnp.sin(entangle_phase))
    stem = lax.all_to_all(stem, "row", 0, 0, tiled=True)
    return batch_last(stem.reshape(batch, parts, block, width))


def solution(mesh):
    return jax.shard_map(
        partial(on_device, rows=mesh.shape["row"], cols=mesh.shape["col"]),
        mesh=mesh,
        in_specs=(P(None, "row", None, "col"), P(("row", "col"), None, None, None, None), P(), P()),
        out_specs=P(None, "row", None, "col"),
        check_vma=False,
    )
```

```python
from functools import partial

import jax
import jax.numpy as jnp
from jax import lax
from jax.experimental import pallas as pl
from jax.experimental.pallas import tpu as pltpu
from jax.sharding import PartitionSpec as P

STEPS = 4
MIB = 1024 * 1024
DOT = partial(jnp.dot, precision=lax.Precision.HIGHEST)


def build_branch(owned):
    left_real, left_imag = (owned[0, 0], owned[0, 1])
    right_real, right_imag = (owned[1, 0], owned[1, 1])
    return jnp.stack(
        [
            DOT(left_real, right_real) - DOT(left_imag, right_imag),
            DOT(left_real, right_imag) + DOT(left_imag, right_real),
        ]
    )


def swap(array, axis, size, bit):
    return lax.ppermute(array, axis, [(i, i ^ bit) for i in range(size)])


def bits_of(size):
    return [1 << i for i in range(size.bit_length() - 1)]


def halve(held, stage):
    axis, size, index, bit = stage
    half = held.shape[0] // 2
    high = (index & bit) // bit
    keep = lax.dynamic_slice_in_dim(held, high * half, half, 0)
    send = lax.dynamic_slice_in_dim(held, (1 - high) * half, half, 0)
    return keep + swap(send, axis, size, bit)


def double(held, stage):
    axis, size, index, bit = stage
    other = swap(held, axis, size, bit)
    high = (index & bit) != 0
    return jnp.concatenate([jnp.where(high, other, held), jnp.where(high, held, other)], 0)


def broadcast_orders(rows, cols):
    row, col = lax.axis_index("row"), lax.axis_index("col")
    row_bits = bits_of(rows)
    first = [("row", rows, row, b) for b in row_bits[:1]]
    along_col = [("col", cols, col, b) for b in bits_of(cols)]
    along_row = [("row", rows, row, b) for b in row_bits[1:2]]
    return first, (along_col + along_row, along_row + along_col), row_bits[2:]


def scatter_branches(own, owners, rows, cols):
    first, orders, _ = broadcast_orders(rows, cols)
    me = lax.axis_index("row") * cols + lax.axis_index("col")
    mine = (owners == me).reshape(STEPS, 1, 1, 1)
    held = jnp.where(mine, own[None], 0.0).reshape(-1, own.shape[-1])
    for stage in first:
        held = halve(held, stage)
    halves = list(jnp.split(held, 2))
    for at in range(len(orders[0])):
        halves = [halve(part, order[at]) for part, order in zip(halves, orders)]
    return jnp.concatenate(halves, 0)


def gather_branches(held, rows, cols):
    first, orders, _ = broadcast_orders(rows, cols)
    halves = list(jnp.split(held, 2))
    for at in reversed(range(len(orders[0]))):
        halves = [double(part, order[at]) for part, order in zip(halves, orders)]
    held = jnp.concatenate(halves, 0)
    for stage in reversed(first):
        held = double(held, stage)
    width = held.shape[-1]
    return held.reshape(STEPS, 2, width, width)


def split(value):
    high = value.astype(jnp.bfloat16)
    low = (value - high.astype(jnp.float32)).astype(jnp.bfloat16)
    return high, low


def prepare_kernel(branch_ref, even_ref, odd_ref):
    for step in range(STEPS):
        real, imag = branch_ref[step, 0], branch_ref[step, 1]
        if step % 2:
            real, imag = real.T, imag.T
        axis = 1 if step % 2 else 0
        (rh, rl), (ih, il) = split(real), split(imag)
        to_real = jnp.concatenate([rh, rh, rl, -ih, -ih, -il], axis)
        to_imag = jnp.concatenate([ih, ih, il, rh, rh, rl], axis)
        out = jnp.concatenate([to_real, to_imag], 1 - axis)
        if step % 2:
            odd_ref[step // 2] = out
        else:
            even_ref[step // 2] = out


def prepare(branches):
    width = branches.shape[-1]
    pairs = STEPS // 2
    return pl.pallas_call(
        prepare_kernel,
        out_shape=(
            jax.ShapeDtypeStruct((pairs, 6 * width, 2 * width), jnp.bfloat16),
            jax.ShapeDtypeStruct((pairs, 2 * width, 6 * width), jnp.bfloat16),
        ),
        compiler_params=pltpu.CompilerParams(vmem_limit_bytes=60 * MIB),
        name="prepare",
    )(branches)


def absorb_kernel(stem_ref, even_ref, odd_ref, cos_ref, sin_ref, out_ref):
    width = cos_ref.shape[1]
    for item in range(stem_ref.shape[1]):
        real = stem_ref[:, item, 0].reshape(width, width)
        imag = stem_ref[:, item, 1].reshape(width, width)
        for step in range(STEPS):
            (rh, rl), (ih, il) = split(real), split(imag)
            if step % 2 == 0:
                stacked = jnp.concatenate([rh, rl, rh, ih, il, ih], 1)
                both = jnp.dot(stacked, even_ref[step // 2], preferred_element_type=jnp.float32)
                real, imag = both[:, :width], both[:, width:]
            else:
                stacked = jnp.concatenate([rh, rl, rh, ih, il, ih], 0)
                both = jnp.dot(odd_ref[step // 2], stacked, preferred_element_type=jnp.float32)
                real, imag = both[:width], both[width:]
            cosine, sine = cos_ref[step], sin_ref[step]
            real, imag = real * cosine - imag * sine, real * sine + imag * cosine
        shape = (stem_ref.shape[0], stem_ref.shape[3], width)
        out_ref[:, item, 0] = real.reshape(shape)
        out_ref[:, item, 1] = imag.reshape(shape)


def absorb(stem, even, odd, cosine, sine):
    peers, items, _, block, width = stem.shape
    spec = pl.BlockSpec((peers, 1, 2, block, width), lambda i: (0, i, 0, 0, 0))
    whole = pl.BlockSpec(memory_space=pltpu.VMEM)
    flops = items * STEPS * 12 * 2 * width**3
    return pl.pallas_call(
        absorb_kernel,
        grid=(items,),
        in_specs=[spec, whole, whole, whole, whole],
        out_specs=spec,
        out_shape=jax.ShapeDtypeStruct(stem.shape, jnp.float32),
        cost_estimate=pl.CostEstimate(flops=flops, bytes_accessed=8 * stem.size, transcendentals=0),
        compiler_params=pltpu.CompilerParams(vmem_limit_bytes=60 * MIB),
        name="absorb",
    )(stem, even, odd, cosine, sine)


def batch_first_kernel(start, stem_ref, out_ref):
    batch = out_ref.shape[0]
    for i in range(stem_ref.shape[1]):
        out_ref[:, 0, i, :] = stem_ref[0, i][:, start : start + batch].T


def batch_first(stem, start, batch):
    parts, rows, width, lanes = stem.shape
    return pl.pallas_call(
        partial(batch_first_kernel, start),
        grid=(parts, rows // 8),
        in_specs=[pl.BlockSpec((1, 8, width, lanes), lambda p, r: (p, r, 0, 0))],
        out_specs=pl.BlockSpec((batch, 1, 8, width), lambda p, r: (0, p, r, 0)),
        out_shape=jax.ShapeDtypeStruct((batch, parts, rows, width), jnp.float32),
        cost_estimate=pl.CostEstimate(flops=0, bytes_accessed=8 * stem.size, transcendentals=0),
        compiler_params=pltpu.CompilerParams(vmem_limit_bytes=60 * MIB),
        name="batch_first",
    )(stem)


def rows_first_kernel(stem_ref, out_ref):
    for i in range(out_ref.shape[1]):
        out_ref[0, i] = stem_ref[:, 0, i, :]


def rows_first(stem):
    batch, parts, rows, width = stem.shape
    return pl.pallas_call(
        rows_first_kernel,
        grid=(parts, rows // 8),
        in_specs=[pl.BlockSpec((batch, 1, 8, width), lambda p, r: (0, p, r, 0))],
        out_specs=pl.BlockSpec((1, 8, batch, width), lambda p, r: (p, r, 0, 0)),
        out_shape=jax.ShapeDtypeStruct((parts, rows, batch, width), jnp.float32),
        cost_estimate=pl.CostEstimate(flops=0, bytes_accessed=8 * stem.size, transcendentals=0),
        compiler_params=pltpu.CompilerParams(vmem_limit_bytes=60 * MIB),
        name="rows_first",
    )(stem)


def batch_last_kernel(low_ref, high_ref, out_ref):
    low = low_ref.shape[2]
    for i in range(out_ref.shape[1]):
        out_ref[0, i, :, :low] = low_ref[0, i].T
        out_ref[0, i, :, low:] = high_ref[:, 0, i, :].T


def batch_last(low, high):
    parts, rows, low_batch, width = low.shape
    high_batch = high.shape[0]
    batch = low_batch + high_batch
    return pl.pallas_call(
        batch_last_kernel,
        grid=(parts, rows // 8),
        in_specs=[
            pl.BlockSpec((1, 8, low_batch, width), lambda p, r: (p, r, 0, 0)),
            pl.BlockSpec((high_batch, 1, 8, width), lambda p, r: (0, p, r, 0)),
        ],
        out_specs=pl.BlockSpec((1, 8, width, batch), lambda p, r: (p, r, 0, 0)),
        out_shape=jax.ShapeDtypeStruct((parts, rows, width, batch), jnp.float32),
        compiler_params=pltpu.CompilerParams(vmem_limit_bytes=60 * MIB),
        name="batch_last",
    )(low, high)


def exchange(parts):
    return lax.all_to_all(parts, "row", 0, 0, tiled=True)


def on_device(stem_slab, factors, branch_owner, entangle_phase, *, rows, cols):
    parts, block, width, batch = stem_slab.shape
    items = batch // rows
    low = max(1, items // 4)
    high = items - low
    sent_low = batch_first(stem_slab, 0, rows * low).reshape(rows, low, parts, block, width)
    sent_low, factors = lax.optimization_barrier((sent_low, factors))
    stem_low = exchange(sent_low)
    held = scatter_branches(build_branch(factors[0]), branch_owner, rows, cols)
    cosine, sine = jnp.cos(entangle_phase), jnp.sin(entangle_phase)
    for bit in broadcast_orders(rows, cols)[2]:
        held = held + swap(held, "row", rows, bit)
    sent_high = batch_first(stem_slab, rows * low, rows * high).reshape(rows, high, parts, block, width)
    held, sent_high, cosine, sine = lax.optimization_barrier((held, sent_high, cosine, sine))
    stem_high = exchange(sent_high)
    even, odd = prepare(gather_branches(held, rows, cols))
    back_low = exchange(absorb(stem_low, even, odd, cosine, sine))
    back_high = exchange(absorb(stem_high, even, odd, cosine, sine))
    back_low = rows_first(back_low.reshape(rows * low, parts, block, width))
    return batch_last(back_low, back_high.reshape(rows * high, parts, block, width))


def solution(mesh):
    return jax.shard_map(
        partial(on_device, rows=mesh.shape["row"], cols=mesh.shape["col"]),
        mesh=mesh,
        in_specs=(P(None, "row", None, "col"), P(("row", "col"), None, None, None, None), P(), P()),
        out_specs=P(None, "row", None, "col"),
        check_vma=False,
    )
```

```python
from functools import partial

import jax
import jax.numpy as jnp
from jax import lax
from jax.experimental import pallas as pl
from jax.experimental.pallas import tpu as pltpu
from jax.sharding import PartitionSpec as P

STEPS = 4
MIB = 1024 * 1024
DOT = partial(jnp.dot, precision=lax.Precision.HIGHEST)


def build_branch(owned):
    left_real, left_imag = (owned[0, 0], owned[0, 1])
    right_real, right_imag = (owned[1, 0], owned[1, 1])
    return jnp.stack(
        [
            DOT(left_real, right_real) - DOT(left_imag, right_imag),
            DOT(left_real, right_imag) + DOT(left_imag, right_real),
        ]
    )


def swap(array, axis, size, bit):
    return lax.ppermute(array, axis, [(i, i ^ bit) for i in range(size)])


def bits_of(size):
    return [1 << i for i in range(size.bit_length() - 1)]


def halve(held, stage):
    axis, size, index, bit = stage
    half = held.shape[0] // 2
    high = (index & bit) // bit
    keep = lax.dynamic_slice_in_dim(held, high * half, half, 0)
    send = lax.dynamic_slice_in_dim(held, (1 - high) * half, half, 0)
    return keep + swap(send, axis, size, bit)


def double(held, stage):
    axis, size, index, bit = stage
    other = swap(held, axis, size, bit)
    high = (index & bit) != 0
    return jnp.concatenate([jnp.where(high, other, held), jnp.where(high, held, other)], 0)


def broadcast_orders(rows, cols):
    row, col = lax.axis_index("row"), lax.axis_index("col")
    row_bits = bits_of(rows)
    first = [("row", rows, row, b) for b in row_bits[:1]]
    along_col = [("col", cols, col, b) for b in bits_of(cols)]
    along_row = [("row", rows, row, b) for b in row_bits[1:2]]
    return first, (along_col + along_row, along_row + along_col), row_bits[2:]


def scatter_branches(own, owners, rows, cols):
    first, orders, _ = broadcast_orders(rows, cols)
    me = lax.axis_index("row") * cols + lax.axis_index("col")
    mine = (owners == me).reshape(STEPS, 1, 1, 1)
    held = jnp.where(mine, own[None], 0.0).reshape(-1, own.shape[-1])
    for stage in first:
        held = halve(held, stage)
    halves = list(jnp.split(held, 2))
    for at in range(len(orders[0])):
        halves = [halve(part, order[at]) for part, order in zip(halves, orders)]
    return jnp.concatenate(halves, 0)


def gather_branches(held, rows, cols):
    first, orders, _ = broadcast_orders(rows, cols)
    halves = list(jnp.split(held, 2))
    for at in reversed(range(len(orders[0]))):
        halves = [double(part, order[at]) for part, order in zip(halves, orders)]
    held = jnp.concatenate(halves, 0)
    for stage in reversed(first):
        held = double(held, stage)
    width = held.shape[-1]
    return held.reshape(STEPS, 2, width, width)


def split(value):
    high = value.astype(jnp.bfloat16)
    low = (value - high.astype(jnp.float32)).astype(jnp.bfloat16)
    return high, low


def stack_branches(branch_ref, even_ref, odd_ref):
    for step in range(STEPS):
        real, imag = branch_ref[step, 0], branch_ref[step, 1]
        if step % 2:
            real, imag = real.T, imag.T
        axis = 1 if step % 2 else 0
        (rh, rl), (ih, il) = split(real), split(imag)
        to_real = jnp.concatenate([rh, rh, rl, -ih, -ih, -il], axis)
        to_imag = jnp.concatenate([ih, ih, il, rh, rh, rl], axis)
        out = jnp.concatenate([to_real, to_imag], 1 - axis)
        if step % 2:
            odd_ref[step // 2] = out
        else:
            even_ref[step // 2] = out


def absorb_kernel(stem_ref, branch_ref, cos_ref, sin_ref, out_ref, even_ref, odd_ref):
    width = cos_ref.shape[1]

    @pl.when(pl.program_id(0) == 0)
    def _():
        stack_branches(branch_ref, even_ref, odd_ref)

    for item in range(stem_ref.shape[1]):
        real = stem_ref[:, item, 0].reshape(width, width)
        imag = stem_ref[:, item, 1].reshape(width, width)
        for step in range(STEPS):
            (rh, rl), (ih, il) = split(real), split(imag)
            if step % 2 == 0:
                stacked = jnp.concatenate([rh, rl, rh, ih, il, ih], 1)
                both = jnp.dot(stacked, even_ref[step // 2], preferred_element_type=jnp.float32)
                real, imag = both[:, :width], both[:, width:]
            else:
                stacked = jnp.concatenate([rh, rl, rh, ih, il, ih], 0)
                both = jnp.dot(odd_ref[step // 2], stacked, preferred_element_type=jnp.float32)
                real, imag = both[:width], both[width:]
            cosine, sine = cos_ref[step], sin_ref[step]
            real, imag = real * cosine - imag * sine, real * sine + imag * cosine
        shape = (stem_ref.shape[0], stem_ref.shape[3], width)
        out_ref[:, item, 0] = real.reshape(shape)
        out_ref[:, item, 1] = imag.reshape(shape)


def in_hbm(*arrays):
    return [pltpu.with_memory_space_constraint(array, pltpu.HBM) for array in arrays]


def whole(array):
    return pl.BlockSpec(array.shape, lambda i: (0,) * array.ndim, pipeline_mode=pl.Buffered(1))


def absorb(stem, branches, cosine, sine):
    peers, items, _, block, width = stem.shape
    per = 2 if items % 2 == 0 else 1
    spec = pl.BlockSpec((peers, per, 2, block, width), lambda i: (0, i, 0, 0, 0))
    flops = items * STEPS * 12 * 2 * width**3
    return pl.pallas_call(
        absorb_kernel,
        grid=(items // per,),
        in_specs=[spec, whole(branches), whole(cosine), whole(sine)],
        out_specs=spec,
        out_shape=pltpu.HBM(stem.shape, jnp.float32),
        scratch_shapes=[
            pltpu.VMEM((STEPS // 2, 6 * width, 2 * width), jnp.bfloat16),
            pltpu.VMEM((STEPS // 2, 2 * width, 6 * width), jnp.bfloat16),
        ],
        cost_estimate=pl.CostEstimate(flops=flops, bytes_accessed=8 * stem.size, transcendentals=0),
        compiler_params=pltpu.CompilerParams(vmem_limit_bytes=32 * MIB),
        name="absorb",
    )(*in_hbm(stem, branches, cosine, sine))


def row_groups(parts, rows):
    return [(part, row) for part in range(parts) for row in range(0, rows, 8)]


def batch_first_kernel(start, stem_ref, out_ref, held, made, in_sem, out_sem):
    parts, rows = stem_ref.shape[:2]
    batch = out_ref.shape[0]
    ins, outs = [], []
    for g, (part, row) in enumerate(row_groups(parts, rows)):
        ins.append(pltpu.make_async_copy(stem_ref.at[part, pl.ds(row, 8)], held.at[g], in_sem.at[g]))
        outs.append(pltpu.make_async_copy(made.at[g], out_ref.at[:, part, pl.ds(row, 8), :], out_sem.at[g]))
    for copy in ins:
        copy.start()
    for g, copy in enumerate(ins):
        copy.wait()
        for i in range(8):
            made[g, :, i, :] = held[g, i][:, start : start + batch].T
        outs[g].start()
    for copy in outs:
        copy.wait()


def batch_first(stem, start, batch):
    parts, rows, width, lanes = stem.shape
    groups = parts * rows // 8
    return pl.pallas_call(
        partial(batch_first_kernel, start),
        in_specs=[pl.BlockSpec(memory_space=pl.ANY)],
        out_specs=pl.BlockSpec(memory_space=pl.ANY),
        out_shape=pltpu.HBM((batch, parts, rows, width), jnp.float32),
        scratch_shapes=[
            pltpu.VMEM((groups, 8, width, lanes), jnp.float32),
            pltpu.VMEM((groups, batch, 8, width), jnp.float32),
            pltpu.SemaphoreType.DMA((groups,)),
            pltpu.SemaphoreType.DMA((groups,)),
        ],
        cost_estimate=pl.CostEstimate(flops=0, bytes_accessed=8 * stem.size, transcendentals=0),
        compiler_params=pltpu.CompilerParams(vmem_limit_bytes=24 * MIB),
        name="batch_first",
    )(*in_hbm(stem))


def rows_first_kernel(stem_ref, out_ref):
    for i in range(out_ref.shape[1]):
        out_ref[0, i] = stem_ref[:, 0, i, :]


def rows_first(stem):
    batch, parts, rows, width = stem.shape
    return pl.pallas_call(
        rows_first_kernel,
        grid=(parts, rows // 8),
        in_specs=[pl.BlockSpec((batch, 1, 8, width), lambda p, r: (0, p, r, 0))],
        out_specs=pl.BlockSpec((1, 8, batch, width), lambda p, r: (p, r, 0, 0)),
        out_shape=pltpu.HBM((parts, rows, batch, width), jnp.float32),
        cost_estimate=pl.CostEstimate(flops=0, bytes_accessed=8 * stem.size, transcendentals=0),
        compiler_params=pltpu.CompilerParams(vmem_limit_bytes=24 * MIB),
        name="rows_first",
    )(*in_hbm(stem))


def batch_last_kernel(low_ref, high_ref, out_ref, low, made, low_sem, out_sem):
    parts, rows = out_ref.shape[:2]
    ins, outs = [], []
    for g, (part, row) in enumerate(row_groups(parts, rows)):
        ins.append(pltpu.make_async_copy(low_ref.at[part, pl.ds(row, 8)], low.at[g], low_sem.at[g]))
        outs.append(pltpu.make_async_copy(made.at[g], out_ref.at[part, pl.ds(row, 8)], out_sem.at[g]))
    for copy in ins:
        copy.start()
    for g, (part, row) in enumerate(row_groups(parts, rows)):
        ins[g].wait()
        for i in range(8):
            made[g, i] = jnp.concatenate([low[g, i], high_ref[:, part, row + i, :]], 0).T
        outs[g].start()
    for copy in outs:
        copy.wait()


def batch_last(low, high):
    parts, rows, low_batch, width = low.shape
    high_batch = high.shape[0]
    batch = low_batch + high_batch
    groups = parts * rows // 8
    return pl.pallas_call(
        batch_last_kernel,
        in_specs=[pl.BlockSpec(memory_space=pl.ANY), pl.BlockSpec(memory_space=pltpu.VMEM)],
        out_specs=pl.BlockSpec(memory_space=pl.ANY),
        out_shape=jax.ShapeDtypeStruct((parts, rows, width, batch), jnp.float32),
        scratch_shapes=[
            pltpu.VMEM((groups, 8, low_batch, width), jnp.float32),
            pltpu.VMEM((groups, 8, width, batch), jnp.float32),
            pltpu.SemaphoreType.DMA((groups,)),
            pltpu.SemaphoreType.DMA((groups,)),
        ],
        compiler_params=pltpu.CompilerParams(vmem_limit_bytes=24 * MIB),
        name="batch_last",
    )(*in_hbm(low), high)


def exchange(parts):
    return lax.all_to_all(parts, "row", 0, 0, tiled=True)


def on_device(stem_slab, factors, branch_owner, entangle_phase, *, rows, cols):
    parts, block, width, batch = stem_slab.shape
    items = batch // rows
    low = max(1, items * 3 // 8)
    high = items - low
    sent_low = batch_first(stem_slab, 0, rows * low).reshape(rows, low, parts, block, width)
    sent_low, factors = lax.optimization_barrier((sent_low, factors))
    stem_low = exchange(sent_low)
    held = scatter_branches(build_branch(factors[0]), branch_owner, rows, cols)
    cosine, sine = jnp.cos(entangle_phase), jnp.sin(entangle_phase)
    for bit in broadcast_orders(rows, cols)[2]:
        held = held + swap(held, "row", rows, bit)
    sent_high = batch_first(stem_slab, rows * low, rows * high).reshape(rows, high, parts, block, width)
    held, sent_high, cosine, sine = lax.optimization_barrier((held, sent_high, cosine, sine))
    stem_high = exchange(sent_high)
    branches = gather_branches(held, rows, cols)
    back_low = exchange(absorb(stem_low, branches, cosine, sine))
    back_high = exchange(absorb(stem_high, branches, cosine, sine))
    back_low = rows_first(back_low.reshape(rows * low, parts, block, width))
    return batch_last(back_low, back_high.reshape(rows * high, parts, block, width))


def solution(mesh):
    return jax.shard_map(
        partial(on_device, rows=mesh.shape["row"], cols=mesh.shape["col"]),
        mesh=mesh,
        in_specs=(P(None, "row", None, "col"), P(("row", "col"), None, None, None, None), P(), P()),
        out_specs=P(None, "row", None, "col"),
        check_vma=False,
    )
```

```python
from functools import partial

import jax
import jax.numpy as jnp
from jax import lax
from jax.experimental import pallas as pl
from jax.experimental.pallas import tpu as pltpu
from jax.sharding import PartitionSpec as P

STEPS = 4
MIB = 1024 * 1024
WEIGHT = 3.35
DOT = partial(jnp.dot, precision=lax.Precision.HIGHEST)


def build_branch(owned):
    left_real, left_imag = (owned[0, 0], owned[0, 1])
    right_real, right_imag = (owned[1, 0], owned[1, 1])
    return jnp.stack(
        [
            DOT(left_real, right_real) - DOT(left_imag, right_imag),
            DOT(left_real, right_imag) + DOT(left_imag, right_real),
        ]
    )


def swap(array, axis, size, bit):
    return lax.ppermute(array, axis, [(i, i ^ bit) for i in range(size)])


def bits_of(size):
    return [1 << i for i in range(size.bit_length() - 1)]


def halve(held, stage):
    axis, size, index, bit = stage
    half = held.shape[0] // 2
    high = (index & bit) // bit
    keep = lax.dynamic_slice_in_dim(held, high * half, half, 0)
    send = lax.dynamic_slice_in_dim(held, (1 - high) * half, half, 0)
    return keep + swap(send, axis, size, bit)


def double(held, stage):
    axis, size, index, bit = stage
    other = swap(held, axis, size, bit)
    high = (index & bit) != 0
    return jnp.concatenate([jnp.where(high, other, held), jnp.where(high, held, other)], 0)


def broadcast_orders(rows, cols):
    row, col = lax.axis_index("row"), lax.axis_index("col")
    row_bits = bits_of(rows)
    first = [("row", rows, row, b) for b in row_bits[:1]]
    along_col = [("col", cols, col, b) for b in bits_of(cols)]
    along_row = [("row", rows, row, b) for b in row_bits[1:2]]
    return first, (along_col + along_row, along_row + along_col), row_bits[2:]


def scatter_branches(own, owners, rows, cols):
    first, orders, _ = broadcast_orders(rows, cols)
    me = lax.axis_index("row") * cols + lax.axis_index("col")
    mine = (owners == me).reshape(STEPS, 1, 1, 1)
    held = jnp.where(mine, own[None], 0.0).reshape(-1, own.shape[-1])
    for stage in first:
        held = halve(held, stage)
    halves = list(jnp.split(held, 2))
    for at in range(len(orders[0])):
        halves = [halve(part, order[at]) for part, order in zip(halves, orders)]
    return jnp.concatenate(halves, 0)


def gather_branches(held, rows, cols):
    first, orders, _ = broadcast_orders(rows, cols)
    halves = list(jnp.split(held, 2))
    for at in reversed(range(len(orders[0]))):
        halves = [double(part, order[at]) for part, order in zip(halves, orders)]
    held = jnp.concatenate(halves, 0)
    for stage in reversed(first):
        held = double(held, stage)
    width = held.shape[-1]
    return held.reshape(STEPS, 2, width, width)


def split(value):
    high = value.astype(jnp.bfloat16)
    low = (value - high.astype(jnp.float32)).astype(jnp.bfloat16)
    return high, low


def stack_branches(branch_ref, even_ref, odd_ref):
    for step in range(STEPS):
        real, imag = branch_ref[step, 0], branch_ref[step, 1]
        if step % 2:
            real, imag = real.T, imag.T
        axis = 1 if step % 2 else 0
        (rh, rl), (ih, il) = split(real), split(imag)
        to_real = jnp.concatenate([rh, rh, rl, -ih, -ih, -il], axis)
        to_imag = jnp.concatenate([ih, ih, il, rh, rh, rl], axis)
        out = jnp.concatenate([to_real, to_imag], 1 - axis)
        if step % 2:
            odd_ref[step // 2] = out
        else:
            even_ref[step // 2] = out


def absorb_kernel(stem_ref, branch_ref, cos_ref, sin_ref, out_ref, even_ref, odd_ref):
    width = cos_ref.shape[1]

    @pl.when(pl.program_id(0) == 0)
    def _():
        stack_branches(branch_ref, even_ref, odd_ref)

    for item in range(stem_ref.shape[1]):
        real = stem_ref[:, item, 0].reshape(width, width)
        imag = stem_ref[:, item, 1].reshape(width, width)
        for step in range(STEPS):
            (rh, rl), (ih, il) = split(real), split(imag)
            if step % 2 == 0:
                stacked = jnp.concatenate([rh, rl, rh, ih, il, ih], 1)
                both = jnp.dot(stacked, even_ref[step // 2], preferred_element_type=jnp.float32)
                real, imag = both[:, :width], both[:, width:]
            else:
                stacked = jnp.concatenate([rh, rl, rh, ih, il, ih], 0)
                both = jnp.dot(odd_ref[step // 2], stacked, preferred_element_type=jnp.float32)
                real, imag = both[:width], both[width:]
            cosine, sine = cos_ref[step], sin_ref[step]
            real, imag = real * cosine - imag * sine, real * sine + imag * cosine
        shape = (stem_ref.shape[0], stem_ref.shape[3], width)
        out_ref[:, item, 0] = real.reshape(shape)
        out_ref[:, item, 1] = imag.reshape(shape)


def in_hbm(*arrays):
    return [pltpu.with_memory_space_constraint(array, pltpu.HBM) for array in arrays]


def whole(array):
    return pl.BlockSpec(array.shape, lambda i: (0,) * array.ndim, pipeline_mode=pl.Buffered(1))


def absorb(stem, branches, cosine, sine, weight=1):
    peers, items, _, block, width = stem.shape
    per = 2 if items % 2 == 0 else 1
    spec = pl.BlockSpec((peers, per, 2, block, width), lambda i: (0, i, 0, 0, 0))
    flops = items * STEPS * 12 * 2 * width**3
    return pl.pallas_call(
        absorb_kernel,
        grid=(items // per,),
        in_specs=[spec, whole(branches), whole(cosine), whole(sine)],
        out_specs=spec,
        out_shape=pltpu.HBM(stem.shape, jnp.float32),
        scratch_shapes=[
            pltpu.VMEM((STEPS // 2, 6 * width, 2 * width), jnp.bfloat16),
            pltpu.VMEM((STEPS // 2, 2 * width, 6 * width), jnp.bfloat16),
        ],
        cost_estimate=pl.CostEstimate(flops=int(flops * weight), bytes_accessed=8 * stem.size, transcendentals=0),
        compiler_params=pltpu.CompilerParams(vmem_limit_bytes=32 * MIB),
        name="absorb",
    )(*in_hbm(stem, branches, cosine, sine))


def row_groups(parts, rows):
    return [(part, row) for part in range(parts) for row in range(0, rows, 8)]


def batch_first_kernel(start, stem_ref, out_ref, held, made, in_sem, out_sem):
    parts, rows = stem_ref.shape[:2]
    batch = out_ref.shape[0]
    ins, outs = [], []
    for g, (part, row) in enumerate(row_groups(parts, rows)):
        ins.append(pltpu.make_async_copy(stem_ref.at[part, pl.ds(row, 8)], held.at[g], in_sem.at[g]))
        outs.append(pltpu.make_async_copy(made.at[g], out_ref.at[:, part, pl.ds(row, 8), :], out_sem.at[g]))
    for copy in ins:
        copy.start()
    for g, copy in enumerate(ins):
        copy.wait()
        for i in range(8):
            made[g, :, i, :] = held[g, i][:, start : start + batch].T
        outs[g].start()
    for copy in outs:
        copy.wait()


def batch_first(stem, start, batch):
    parts, rows, width, lanes = stem.shape
    groups = parts * rows // 8
    return pl.pallas_call(
        partial(batch_first_kernel, start),
        in_specs=[pl.BlockSpec(memory_space=pl.ANY)],
        out_specs=pl.BlockSpec(memory_space=pl.ANY),
        out_shape=pltpu.HBM((batch, parts, rows, width), jnp.float32),
        scratch_shapes=[
            pltpu.VMEM((groups, 8, width, lanes), jnp.float32),
            pltpu.VMEM((groups, batch, 8, width), jnp.float32),
            pltpu.SemaphoreType.DMA((groups,)),
            pltpu.SemaphoreType.DMA((groups,)),
        ],
        cost_estimate=pl.CostEstimate(flops=0, bytes_accessed=8 * stem.size, transcendentals=0),
        compiler_params=pltpu.CompilerParams(vmem_limit_bytes=24 * MIB),
        name="batch_first",
    )(*in_hbm(stem))


def rows_first_kernel(stem_ref, out_ref):
    for i in range(out_ref.shape[1]):
        out_ref[0, i] = stem_ref[:, 0, i, :]


def rows_first(stem):
    batch, parts, rows, width = stem.shape
    return pl.pallas_call(
        rows_first_kernel,
        grid=(parts, rows // 8),
        in_specs=[pl.BlockSpec((batch, 1, 8, width), lambda p, r: (0, p, r, 0))],
        out_specs=pl.BlockSpec((1, 8, batch, width), lambda p, r: (p, r, 0, 0)),
        out_shape=pltpu.HBM((parts, rows, batch, width), jnp.float32),
        cost_estimate=pl.CostEstimate(flops=0, bytes_accessed=8 * stem.size, transcendentals=0),
        compiler_params=pltpu.CompilerParams(vmem_limit_bytes=24 * MIB),
        name="rows_first",
    )(*in_hbm(stem))


def batch_last_kernel(low_ref, high_ref, out_ref, low, made, low_sem, out_sem):
    parts, rows = out_ref.shape[:2]
    ins, outs = [], []
    for g, (part, row) in enumerate(row_groups(parts, rows)):
        ins.append(pltpu.make_async_copy(low_ref.at[part, pl.ds(row, 8)], low.at[g], low_sem.at[g]))
        outs.append(pltpu.make_async_copy(made.at[g], out_ref.at[part, pl.ds(row, 8)], out_sem.at[g]))
    for copy in ins:
        copy.start()
    for g, (part, row) in enumerate(row_groups(parts, rows)):
        ins[g].wait()
        for i in range(8):
            made[g, i] = jnp.concatenate([low[g, i], high_ref[:, part, row + i, :]], 0).T
        outs[g].start()
    for copy in outs:
        copy.wait()


def batch_last(low, high):
    parts, rows, low_batch, width = low.shape
    high_batch = high.shape[0]
    batch = low_batch + high_batch
    groups = parts * rows // 8
    return pl.pallas_call(
        batch_last_kernel,
        in_specs=[pl.BlockSpec(memory_space=pl.ANY), pl.BlockSpec(memory_space=pltpu.VMEM)],
        out_specs=pl.BlockSpec(memory_space=pl.ANY),
        out_shape=jax.ShapeDtypeStruct((parts, rows, width, batch), jnp.float32),
        scratch_shapes=[
            pltpu.VMEM((groups, 8, low_batch, width), jnp.float32),
            pltpu.VMEM((groups, 8, width, batch), jnp.float32),
            pltpu.SemaphoreType.DMA((groups,)),
            pltpu.SemaphoreType.DMA((groups,)),
        ],
        compiler_params=pltpu.CompilerParams(vmem_limit_bytes=24 * MIB),
        name="batch_last",
    )(*in_hbm(low), high)


def exchange(parts):
    return lax.all_to_all(parts, "row", 0, 0, tiled=True)


def on_device(stem_slab, factors, branch_owner, entangle_phase, *, rows, cols):
    parts, block, width, batch = stem_slab.shape
    items = batch // rows
    low = max(1, items * 3 // 8)
    high = items - low
    sent_low = batch_first(stem_slab, 0, rows * low).reshape(rows, low, parts, block, width)
    sent_low, factors = lax.optimization_barrier((sent_low, factors))
    stem_low = exchange(sent_low)
    held = scatter_branches(build_branch(factors[0]), branch_owner, rows, cols)
    cosine, sine = jnp.cos(entangle_phase), jnp.sin(entangle_phase)
    far = broadcast_orders(rows, cols)[2]
    for bit in far[:-1]:
        held = held + swap(held, "row", rows, bit)
    sent_high = batch_first(stem_slab, rows * low, rows * high).reshape(rows, high, parts, block, width)
    held, sent_high, cosine, sine = lax.optimization_barrier((held, sent_high, cosine, sine))
    for bit in far[-1:]:
        held = held + swap(held, "row", rows, bit)
    stem_high = exchange(sent_high)
    branches = gather_branches(held, rows, cols)
    back_low = exchange(absorb(stem_low, branches, cosine, sine, WEIGHT))
    back_high = exchange(absorb(stem_high, branches, cosine, sine))
    back_low = rows_first(back_low.reshape(rows * low, parts, block, width))
    return batch_last(back_low, back_high.reshape(rows * high, parts, block, width))


def solution(mesh):
    return jax.shard_map(
        partial(on_device, rows=mesh.shape["row"], cols=mesh.shape["col"]),
        mesh=mesh,
        in_specs=(P(None, "row", None, "col"), P(("row", "col"), None, None, None, None), P(), P()),
        out_specs=P(None, "row", None, "col"),
        check_vma=False,
    )
```

```python
from functools import partial

import jax
import jax.numpy as jnp
from jax import lax
from jax.experimental import pallas as pl
from jax.experimental.pallas import tpu as pltpu
from jax.sharding import PartitionSpec as P

STEPS = 4
MIB = 1024 * 1024
WEIGHT = 4.5
LAST = 48
PER = (1, 2, 3)
DOT = partial(jnp.dot, precision=lax.Precision.HIGHEST)


def build_branch(owned):
    left_real, left_imag = (owned[0, 0], owned[0, 1])
    right_real, right_imag = (owned[1, 0], owned[1, 1])
    return jnp.stack(
        [
            DOT(left_real, right_real) - DOT(left_imag, right_imag),
            DOT(left_real, right_imag) + DOT(left_imag, right_real),
        ]
    )


def swap(array, axis, size, bit):
    return lax.ppermute(array, axis, [(i, i ^ bit) for i in range(size)])


def bits_of(size):
    return [1 << i for i in range(size.bit_length() - 1)]


def halve(held, stage):
    axis, size, index, bit = stage
    half = held.shape[0] // 2
    high = (index & bit) // bit
    keep = lax.dynamic_slice_in_dim(held, high * half, half, 0)
    send = lax.dynamic_slice_in_dim(held, (1 - high) * half, half, 0)
    return keep + swap(send, axis, size, bit)


def double(held, stage):
    axis, size, index, bit = stage
    other = swap(held, axis, size, bit)
    high = (index & bit) != 0
    return jnp.concatenate([jnp.where(high, other, held), jnp.where(high, held, other)], 0)


def broadcast_orders(rows, cols):
    row, col = lax.axis_index("row"), lax.axis_index("col")
    row_bits = bits_of(rows)
    first = [("row", rows, row, b) for b in row_bits[:1]]
    along_col = [("col", cols, col, b) for b in bits_of(cols)]
    along_row = [("row", rows, row, b) for b in row_bits[1:2]]
    return first, (along_col + along_row, along_row + along_col), row_bits[2:]


def scatter_branches(own, owners, rows, cols):
    first, orders, _ = broadcast_orders(rows, cols)
    me = lax.axis_index("row") * cols + lax.axis_index("col")
    mine = (owners == me).reshape(STEPS, 1, 1, 1)
    held = jnp.where(mine, own[None], 0.0).reshape(-1, own.shape[-1])
    for stage in first:
        held = halve(held, stage)
    halves = list(jnp.split(held, 2))
    for at in range(len(orders[0])):
        halves = [halve(part, order[at]) for part, order in zip(halves, orders)]
    return jnp.concatenate(halves, 0)


def gather_branches(held, rows, cols):
    first, orders, _ = broadcast_orders(rows, cols)
    halves = list(jnp.split(held, 2))
    for at in reversed(range(len(orders[0]))):
        halves = [double(part, order[at]) for part, order in zip(halves, orders)]
    held = jnp.concatenate(halves, 0)
    ((axis, size, _, bit),) = first
    width = held.shape[-1]
    shape = (STEPS // 2, 2, width, width)
    return held.reshape(shape), swap(held, axis, size, bit).reshape(shape)


def split(value):
    high = value.astype(jnp.bfloat16)
    low = (value - high.astype(jnp.float32)).astype(jnp.bfloat16)
    return high, low


def stack_branches(core, mine_ref, other_ref, even_ref, odd_ref):
    pair = STEPS // 2
    for step in range(STEPS):
        here = core == step // pair
        real, imag = (jnp.where(here, mine_ref[step % pair, i], other_ref[step % pair, i]) for i in range(2))
        if step % 2:
            real, imag = real.T, imag.T
        axis = 1 if step % 2 else 0
        (rh, rl), (ih, il) = split(real), split(imag)
        to_real = jnp.concatenate([rh, rh, rl, -ih, -ih, -il], axis)
        to_imag = jnp.concatenate([ih, ih, il, rh, rh, rl], axis)
        out = jnp.concatenate([to_real, to_imag], 1 - axis)
        if step % 2:
            odd_ref[step // 2] = out
        else:
            even_ref[step // 2] = out


def absorb_kernel(core_ref, stem_ref, mine_ref, other_ref, cos_ref, sin_ref, out_ref, even_ref, odd_ref):
    width = cos_ref.shape[1]
    items = range(stem_ref.shape[1])

    @pl.when(pl.program_id(0) == 0)
    def _():
        stack_branches(core_ref[0], mine_ref, other_ref, even_ref, odd_ref)

    held = [[stem_ref[:, item, i].reshape(width, width) for i in range(2)] for item in items]
    for step in range(STEPS):
        cosine, sine = cos_ref[step], sin_ref[step]
        for item in items:
            (rh, rl), (ih, il) = split(held[item][0]), split(held[item][1])
            if step % 2 == 0:
                stacked = jnp.concatenate([rh, rl, rh, ih, il, ih], 1)
                both = jnp.dot(stacked, even_ref[step // 2], preferred_element_type=jnp.float32)
                real, imag = both[:, :width], both[:, width:]
            else:
                stacked = jnp.concatenate([rh, rl, rh, ih, il, ih], 0)
                both = jnp.dot(odd_ref[step // 2], stacked, preferred_element_type=jnp.float32)
                real, imag = both[:width], both[width:]
            held[item] = [real * cosine - imag * sine, real * sine + imag * cosine]
    shape = (stem_ref.shape[0], stem_ref.shape[3], width)
    for item in items:
        for i in range(2):
            out_ref[:, item, i] = held[item][i].reshape(shape)


def in_hbm(*arrays):
    return [pltpu.with_memory_space_constraint(array, pltpu.HBM) for array in arrays]


def whole(array):
    return pl.BlockSpec(array.shape, lambda i: (0,) * array.ndim, pipeline_mode=pl.Buffered(1))


def absorb(stem, branches, cosine, sine, start=0, count=None, weight=1):
    peers, items, _, block, width = stem.shape
    count = items if count is None else count
    per = max(n for n in PER if count % n == 0 and start % n == 0)
    shape = (peers, per, 2, block, width)
    in_spec = pl.BlockSpec(shape, lambda i: (0, i + start // per, 0, 0, 0))
    out_spec = pl.BlockSpec(shape, lambda i: (0, i, 0, 0, 0))
    flops = count * STEPS * 12 * 2 * width**3
    core = (lax.axis_index("row") % 2).astype(jnp.int32).reshape(1)
    arrays = in_hbm(stem, *branches, cosine, sine)
    return pl.pallas_call(
        absorb_kernel,
        grid=(count // per,),
        in_specs=[pl.BlockSpec(memory_space=pltpu.SMEM), in_spec, *(whole(array) for array in arrays[1:])],
        out_specs=out_spec,
        out_shape=pltpu.HBM((peers, count, 2, block, width), jnp.float32),
        scratch_shapes=[
            pltpu.VMEM((STEPS // 2, 6 * width, 2 * width), jnp.bfloat16),
            pltpu.VMEM((STEPS // 2, 2 * width, 6 * width), jnp.bfloat16),
        ],
        cost_estimate=pl.CostEstimate(
            flops=int(flops * weight), bytes_accessed=8 * count * (stem.size // items), transcendentals=0
        ),
        compiler_params=pltpu.CompilerParams(vmem_limit_bytes=40 * MIB),
        name="absorb",
    )(core, *arrays)


def row_groups(parts, rows):
    return [(part, row) for part in range(parts) for row in range(0, rows, 8)]


def batch_first_kernel(start, stem_ref, out_ref, held, made, in_sem, out_sem):
    parts, rows = stem_ref.shape[:2]
    peers, items = out_ref.shape[:2]
    ins, outs = [], []
    for g, (part, row) in enumerate(row_groups(parts, rows)):
        ins.append(pltpu.make_async_copy(stem_ref.at[part, pl.ds(row, 8)], held.at[g], in_sem.at[g]))
        outs.append(
            [
                pltpu.make_async_copy(
                    made.at[g, pl.ds(item * peers, peers)],
                    out_ref.at[:, item, part, pl.ds(row, 8), :],
                    out_sem.at[g, item],
                )
                for item in range(items)
            ]
        )
    for copy in ins:
        copy.start()
    for g, copy in enumerate(ins):
        copy.wait()
        for i in range(8):
            made[g, :, i, :] = held[g, i][:, start : start + peers * items].T
        for out in outs[g]:
            out.start()
    for group in outs:
        for copy in group:
            copy.wait()


def batch_first(stem, peers, start, items):
    parts, rows, width, lanes = stem.shape
    groups = parts * rows // 8
    return pl.pallas_call(
        partial(batch_first_kernel, start * peers),
        in_specs=[pl.BlockSpec(memory_space=pl.ANY)],
        out_specs=pl.BlockSpec(memory_space=pl.ANY),
        out_shape=pltpu.HBM((peers, items, parts, rows, width), jnp.float32),
        scratch_shapes=[
            pltpu.VMEM((groups, 8, width, lanes), jnp.float32),
            pltpu.VMEM((groups, peers * items, 8, width), jnp.float32),
            pltpu.SemaphoreType.DMA((groups,)),
            pltpu.SemaphoreType.DMA((groups, items)),
        ],
        cost_estimate=pl.CostEstimate(flops=0, bytes_accessed=8 * stem.size, transcendentals=0),
        compiler_params=pltpu.CompilerParams(vmem_limit_bytes=24 * MIB),
        name="batch_first",
    )(*in_hbm(stem))


def rows_first_kernel(stem_ref, out_ref):
    peers, items = stem_ref.shape[:2]
    for i in range(out_ref.shape[1]):
        for item in range(items):
            out_ref[0, i, item * peers : (item + 1) * peers] = stem_ref[:, item, 0, i, :]


def rows_first(stem, weight):
    peers, items, parts, rows, width = stem.shape
    return pl.pallas_call(
        rows_first_kernel,
        grid=(parts, rows // 8),
        in_specs=[pl.BlockSpec((peers, items, 1, 8, width), lambda p, r: (0, 0, p, r, 0))],
        out_specs=pl.BlockSpec((1, 8, peers * items, width), lambda p, r: (p, r, 0, 0)),
        out_shape=pltpu.HBM((parts, rows, peers * items, width), jnp.float32),
        cost_estimate=pl.CostEstimate(flops=int(1e9 * weight), bytes_accessed=8 * stem.size, transcendentals=0),
        compiler_params=pltpu.CompilerParams(vmem_limit_bytes=24 * MIB),
        name="rows_first",
    )(*in_hbm(stem))


def batch_last_kernel(low_ref, *refs):
    *others, out_ref, low, made, low_sem, out_sem = refs
    parts, rows = out_ref.shape[:2]
    ins, outs = [], []
    for g, (part, row) in enumerate(row_groups(parts, rows)):
        ins.append(pltpu.make_async_copy(low_ref.at[part, pl.ds(row, 8)], low.at[g], low_sem.at[g]))
        outs.append(pltpu.make_async_copy(made.at[g], out_ref.at[part, pl.ds(row, 8)], out_sem.at[g]))
    for copy in ins:
        copy.start()
    for g, (part, row) in enumerate(row_groups(parts, rows)):
        ins[g].wait()
        for i in range(8):
            found = [ref[:, item, part, row + i, :] for ref in others for item in range(ref.shape[1])]
            made[g, i] = jnp.concatenate([low[g, i], *found], 0).T
        outs[g].start()
    for copy in outs:
        copy.wait()


def batch_last(low, *others):
    parts, rows, batch, width = low.shape
    lanes = batch + sum(other.shape[0] * other.shape[1] for other in others)
    groups = parts * rows // 8
    return pl.pallas_call(
        batch_last_kernel,
        in_specs=[pl.BlockSpec(memory_space=pl.ANY)] + [pl.BlockSpec(memory_space=pltpu.VMEM)] * len(others),
        out_specs=pl.BlockSpec(memory_space=pl.ANY),
        out_shape=jax.ShapeDtypeStruct((parts, rows, width, lanes), jnp.float32),
        scratch_shapes=[
            pltpu.VMEM((groups, 8, batch, width), jnp.float32),
            pltpu.VMEM((groups, 8, width, lanes), jnp.float32),
            pltpu.SemaphoreType.DMA((groups,)),
            pltpu.SemaphoreType.DMA((groups,)),
        ],
        compiler_params=pltpu.CompilerParams(vmem_limit_bytes=24 * MIB),
        name="batch_last",
    )(*in_hbm(low), *others)


def exchange(parts):
    return lax.all_to_all(parts, "row", 0, 0, tiled=True)


def pair_cores(parts):
    rows = parts.shape[0]
    core = lax.axis_index("row") % 2
    chips = parts.reshape(rows // 2, 2, *parts.shape[1:])
    same = lax.dynamic_index_in_dim(chips, core, 1, keepdims=False)
    other = lax.dynamic_index_in_dim(chips, 1 - core, 1, keepdims=False)
    other = swap(other, "row", rows, 1)
    return jnp.stack([jnp.where(core == 0, same, other), jnp.where(core == 0, other, same)], 1)


def send_chips(parts):
    rows = parts.shape[0]
    chip = lax.axis_index("row") // 2
    pairs = pair_cores(parts)
    pieces = {}
    for bit in reversed(range(1, rows // 2)):
        pieces[bit] = swap(lax.dynamic_index_in_dim(pairs, chip ^ bit, 0), "row", rows, 2 * bit)
    return pairs, pieces


def collect_chips(pairs, pieces):
    chip = lax.axis_index("row") // 2
    for bit, piece in pieces.items():
        pairs = lax.dynamic_update_index_in_dim(pairs, piece, chip ^ bit, 0)
    return pairs.reshape(-1, *pairs.shape[2:])


def on_device(stem_slab, factors, branch_owner, entangle_phase, *, rows, cols):
    items = stem_slab.shape[3] // rows
    low = max(1, items * 3 // 8)
    high = items - low
    sent_low = batch_first(stem_slab, rows, 0, low)
    sent_low, factors = lax.optimization_barrier((sent_low, factors))
    stem_low = exchange(sent_low)
    held = scatter_branches(build_branch(factors[0]), branch_owner, rows, cols)
    cosine, sine = jnp.cos(entangle_phase), jnp.sin(entangle_phase)
    far = broadcast_orders(rows, cols)[2]
    for bit in far[:-1]:
        held = held + swap(held, "row", rows, bit)
    sent_high = batch_first(stem_slab, rows, low, high)
    held, sent_high, cosine, sine = lax.optimization_barrier((held, sent_high, cosine, sine))
    for bit in far[-1:]:
        held = held + swap(held, "row", rows, bit)
    stem_high = exchange(sent_high)
    branches = gather_branches(held, rows, cols)
    back_low = exchange(absorb(stem_low, branches, cosine, sine, weight=WEIGHT))
    pairs, pieces = send_chips(absorb(stem_high, branches, cosine, sine, high - 1, 1))
    back_high = exchange(absorb(stem_high, branches, cosine, sine, 0, high - 1))
    order = list(pieces)
    back_low, *came = lax.optimization_barrier((back_low, *[pieces[bit] for bit in order]))
    back_some = collect_chips(pairs, dict(zip(order, came)))
    return batch_last(rows_first(back_low, LAST), back_high, back_some)


def solution(mesh):
    return jax.shard_map(
        partial(on_device, rows=mesh.shape["row"], cols=mesh.shape["col"]),
        mesh=mesh,
        in_specs=(P(None, "row", None, "col"), P(("row", "col"), None, None, None, None), P(), P()),
        out_specs=P(None, "row", None, "col"),
        check_vma=False,
    )
```

```python
from functools import partial

import jax
import jax.numpy as jnp
from jax import lax
from jax.experimental import pallas as pl
from jax.experimental.pallas import tpu as pltpu
from jax.sharding import PartitionSpec as P

STEPS = 4
MIB = 1024 * 1024
WEIGHT = 4.5
LAST = 48
PER = (1, 2, 3)
DOT = partial(jnp.dot, precision=lax.Precision.HIGHEST)


def build_branch(owned):
    left_real, left_imag = (owned[0, 0], owned[0, 1])
    right_real, right_imag = (owned[1, 0], owned[1, 1])
    return jnp.stack(
        [
            DOT(left_real, right_real) - DOT(left_imag, right_imag),
            DOT(left_real, right_imag) + DOT(left_imag, right_real),
        ]
    )


def swap(array, axis, size, bit):
    return lax.ppermute(array, axis, [(i, i ^ bit) for i in range(size)])


def bits_of(size):
    return [1 << i for i in range(size.bit_length() - 1)]


def halve(held, stage):
    axis, size, index, bit = stage
    half = held.shape[0] // 2
    high = (index & bit) // bit
    keep = lax.dynamic_slice_in_dim(held, high * half, half, 0)
    send = lax.dynamic_slice_in_dim(held, (1 - high) * half, half, 0)
    return keep + swap(send, axis, size, bit)


def double(held, stage):
    axis, size, index, bit = stage
    other = swap(held, axis, size, bit)
    high = (index & bit) != 0
    return jnp.concatenate([jnp.where(high, other, held), jnp.where(high, held, other)], 0)


def broadcast_orders(rows, cols):
    row, col = lax.axis_index("row"), lax.axis_index("col")
    row_bits = bits_of(rows)
    first = [("row", rows, row, b) for b in row_bits[:1]]
    along_col = [("col", cols, col, b) for b in bits_of(cols)]
    along_row = [("row", rows, row, b) for b in row_bits[1:2]]
    return first, (along_col + along_row, along_row + along_col), row_bits[2:]


def scatter_branches(own, owners, rows, cols):
    first, orders, _ = broadcast_orders(rows, cols)
    me = lax.axis_index("row") * cols + lax.axis_index("col")
    mine = (owners == me).reshape(STEPS, 1, 1, 1)
    held = jnp.where(mine, own[None], 0.0).reshape(-1, own.shape[-1])
    for stage in first:
        held = halve(held, stage)
    halves = list(jnp.split(held, 2))
    for at in range(len(orders[0])):
        halves = [halve(part, order[at]) for part, order in zip(halves, orders)]
    return jnp.concatenate(halves, 0)


def gather_branches(held, rows, cols):
    first, orders, _ = broadcast_orders(rows, cols)
    halves = list(jnp.split(held, 2))
    for at in reversed(range(len(orders[0]))):
        halves = [double(part, order[at]) for part, order in zip(halves, orders)]
    held = jnp.concatenate(halves, 0)
    ((axis, size, _, bit),) = first
    width = held.shape[-1]
    shape = (STEPS // 2, 2, width, width)
    return held.reshape(shape), swap(held, axis, size, bit).reshape(shape)


def split(value):
    high = value.astype(jnp.bfloat16)
    low = (value - high.astype(jnp.float32)).astype(jnp.bfloat16)
    return high, low


def stack_branches(core, mine_ref, other_ref, even_ref, odd_ref):
    pair = STEPS // 2
    for step in range(STEPS):
        here = core == step // pair
        real, imag = (jnp.where(here, mine_ref[step % pair, i], other_ref[step % pair, i]) for i in range(2))
        if step % 2:
            real, imag = real.T, imag.T
        axis = 1 if step % 2 else 0
        (rh, rl), (ih, il) = split(real), split(imag)
        to_real = jnp.concatenate([rh, rh, rl, -ih, -ih, -il], axis)
        to_imag = jnp.concatenate([ih, ih, il, rh, rh, rl], axis)
        out = jnp.concatenate([to_real, to_imag], 1 - axis)
        if step % 2:
            odd_ref[step // 2] = out
        else:
            even_ref[step // 2] = out


def absorb_kernel(core_ref, stem_ref, mine_ref, other_ref, cos_ref, sin_ref, out_ref, even_ref, odd_ref):
    width = cos_ref.shape[1]
    items = range(stem_ref.shape[1])

    @pl.when(pl.program_id(0) == 0)
    def _():
        stack_branches(core_ref[0], mine_ref, other_ref, even_ref, odd_ref)

    held = [[stem_ref[:, item, i].reshape(width, width) for i in range(2)] for item in items]
    for step in range(STEPS):
        cosine, sine = cos_ref[step], sin_ref[step]
        for item in items:
            (rh, rl), (ih, il) = split(held[item][0]), split(held[item][1])
            if step % 2 == 0:
                stacked = jnp.concatenate([rh, rl, rh, ih, il, ih], 1)
                both = jnp.dot(stacked, even_ref[step // 2], preferred_element_type=jnp.float32)
                real, imag = both[:, :width], both[:, width:]
            else:
                stacked = jnp.concatenate([rh, rl, rh, ih, il, ih], 0)
                both = jnp.dot(odd_ref[step // 2], stacked, preferred_element_type=jnp.float32)
                real, imag = both[:width], both[width:]
            held[item] = [real * cosine - imag * sine, real * sine + imag * cosine]
    shape = (stem_ref.shape[0], stem_ref.shape[3], width)
    for item in items:
        for i in range(2):
            out_ref[:, item, i] = held[item][i].reshape(shape)


def in_hbm(*arrays):
    return [pltpu.with_memory_space_constraint(array, pltpu.HBM) for array in arrays]


def whole(array):
    return pl.BlockSpec(array.shape, lambda i: (0,) * array.ndim, pipeline_mode=pl.Buffered(1))


def absorb(stem, branches, cosine, sine, start=0, count=None, weight=1):
    peers, items, _, block, width = stem.shape
    count = items if count is None else count
    per = max(n for n in PER if count % n == 0 and start % n == 0)
    shape = (peers, per, 2, block, width)
    in_spec = pl.BlockSpec(shape, lambda i: (0, i + start // per, 0, 0, 0))
    out_spec = pl.BlockSpec(shape, lambda i: (0, i, 0, 0, 0))
    flops = count * STEPS * 12 * 2 * width**3
    core = (lax.axis_index("row") % 2).astype(jnp.int32).reshape(1)
    arrays = in_hbm(stem, *branches, cosine, sine)
    return pl.pallas_call(
        absorb_kernel,
        grid=(count // per,),
        in_specs=[pl.BlockSpec(memory_space=pltpu.SMEM), in_spec, *(whole(array) for array in arrays[1:])],
        out_specs=out_spec,
        out_shape=pltpu.HBM((peers, count, 2, block, width), jnp.float32),
        scratch_shapes=[
            pltpu.VMEM((STEPS // 2, 6 * width, 2 * width), jnp.bfloat16),
            pltpu.VMEM((STEPS // 2, 2 * width, 6 * width), jnp.bfloat16),
        ],
        cost_estimate=pl.CostEstimate(
            flops=int(flops * weight), bytes_accessed=8 * count * (stem.size // items), transcendentals=0
        ),
        compiler_params=pltpu.CompilerParams(vmem_limit_bytes=40 * MIB),
        name="absorb",
    )(core, *arrays)


def row_groups(parts, rows):
    return [(part, row) for part in range(parts) for row in range(0, rows, 8)]


def batch_first_kernel(start, stem_ref, out_ref, held, made, in_sem, out_sem):
    parts, rows = stem_ref.shape[:2]
    peers, items = out_ref.shape[:2]
    ins, outs = [], []
    for g, (part, row) in enumerate(row_groups(parts, rows)):
        ins.append(pltpu.make_async_copy(stem_ref.at[part, pl.ds(row, 8)], held.at[g], in_sem.at[g]))
        outs.append(
            [
                pltpu.make_async_copy(
                    made.at[g, pl.ds(item * peers, peers)],
                    out_ref.at[:, item, part, pl.ds(row, 8), :],
                    out_sem.at[g, item],
                )
                for item in range(items)
            ]
        )
    for copy in ins:
        copy.start()
    for g, copy in enumerate(ins):
        copy.wait()
        for i in range(8):
            made[g, :, i, :] = held[g, i][:, start : start + peers * items].T
        for out in outs[g]:
            out.start()
    for group in outs:
        for copy in group:
            copy.wait()


def batch_first(stem, peers, start, items):
    parts, rows, width, lanes = stem.shape
    groups = parts * rows // 8
    return pl.pallas_call(
        partial(batch_first_kernel, start * peers),
        in_specs=[pl.BlockSpec(memory_space=pl.ANY)],
        out_specs=pl.BlockSpec(memory_space=pl.ANY),
        out_shape=pltpu.HBM((peers, items, parts, rows, width), jnp.float32),
        scratch_shapes=[
            pltpu.VMEM((groups, 8, width, lanes), jnp.float32),
            pltpu.VMEM((groups, peers * items, 8, width), jnp.float32),
            pltpu.SemaphoreType.DMA((groups,)),
            pltpu.SemaphoreType.DMA((groups, items)),
        ],
        cost_estimate=pl.CostEstimate(flops=0, bytes_accessed=8 * stem.size, transcendentals=0),
        compiler_params=pltpu.CompilerParams(vmem_limit_bytes=24 * MIB),
        name="batch_first",
    )(*in_hbm(stem))


def rows_first_kernel(stem_ref, out_ref):
    peers, items = stem_ref.shape[:2]
    for i in range(out_ref.shape[1]):
        for item in range(items):
            out_ref[0, i, item * peers : (item + 1) * peers] = stem_ref[:, item, 0, i, :]


def rows_first(stem, weight):
    peers, items, parts, rows, width = stem.shape
    return pl.pallas_call(
        rows_first_kernel,
        grid=(parts, rows // 8),
        in_specs=[pl.BlockSpec((peers, items, 1, 8, width), lambda p, r: (0, 0, p, r, 0))],
        out_specs=pl.BlockSpec((1, 8, peers * items, width), lambda p, r: (p, r, 0, 0)),
        out_shape=pltpu.HBM((parts, rows, peers * items, width), jnp.float32),
        cost_estimate=pl.CostEstimate(flops=int(1e9 * weight), bytes_accessed=8 * stem.size, transcendentals=0),
        compiler_params=pltpu.CompilerParams(vmem_limit_bytes=24 * MIB),
        name="rows_first",
    )(*in_hbm(stem))


def batch_last_kernel(low_ref, *refs):
    *others, out_ref, low, made, low_sem, out_sem = refs
    parts, rows = out_ref.shape[:2]
    ins, outs = [], []
    for g, (part, row) in enumerate(row_groups(parts, rows)):
        ins.append(pltpu.make_async_copy(low_ref.at[part, pl.ds(row, 8)], low.at[g], low_sem.at[g]))
        outs.append(pltpu.make_async_copy(made.at[g], out_ref.at[part, pl.ds(row, 8)], out_sem.at[g]))
    for copy in ins:
        copy.start()
    for g, (part, row) in enumerate(row_groups(parts, rows)):
        ins[g].wait()
        for i in range(8):
            found = [ref[:, item, part, row + i, :] for ref in others for item in range(ref.shape[1])]
            made[g, i] = jnp.concatenate([low[g, i], *found], 0).T
        outs[g].start()
    for copy in outs:
        copy.wait()


def batch_last(low, *others):
    parts, rows, batch, width = low.shape
    lanes = batch + sum(other.shape[0] * other.shape[1] for other in others)
    groups = parts * rows // 8
    return pl.pallas_call(
        batch_last_kernel,
        in_specs=[pl.BlockSpec(memory_space=pl.ANY)] + [pl.BlockSpec(memory_space=pltpu.VMEM)] * len(others),
        out_specs=pl.BlockSpec(memory_space=pl.ANY),
        out_shape=jax.ShapeDtypeStruct((parts, rows, width, lanes), jnp.float32),
        scratch_shapes=[
            pltpu.VMEM((groups, 8, batch, width), jnp.float32),
            pltpu.VMEM((groups, 8, width, lanes), jnp.float32),
            pltpu.SemaphoreType.DMA((groups,)),
            pltpu.SemaphoreType.DMA((groups,)),
        ],
        compiler_params=pltpu.CompilerParams(vmem_limit_bytes=24 * MIB),
        name="batch_last",
    )(*in_hbm(low), *others)


def exchange(parts):
    return lax.all_to_all(parts, "row", 0, 0, tiled=True)


def pair_cores(parts):
    rows = parts.shape[0]
    core = lax.axis_index("row") % 2
    chips = parts.reshape(rows // 2, 2, *parts.shape[1:])
    same = lax.dynamic_index_in_dim(chips, core, 1, keepdims=False)
    other = lax.dynamic_index_in_dim(chips, 1 - core, 1, keepdims=False)
    other = swap(other, "row", rows, 1)
    return jnp.stack([jnp.where(core == 0, same, other), jnp.where(core == 0, other, same)], 1)


def send_chips(parts):
    rows = parts.shape[0]
    chip = lax.axis_index("row") // 2
    pairs = pair_cores(parts)
    pieces = {}
    for bit in reversed(range(1, rows // 2)):
        pieces[bit] = swap(lax.dynamic_index_in_dim(pairs, chip ^ bit, 0), "row", rows, 2 * bit)
    return pairs, pieces


def collect_chips(pairs, pieces):
    chip = lax.axis_index("row") // 2
    for bit, piece in pieces.items():
        pairs = lax.dynamic_update_index_in_dim(pairs, piece, chip ^ bit, 0)
    return pairs.reshape(-1, *pairs.shape[2:])


def on_device(stem_slab, factors, branch_owner, entangle_phase, *, rows, cols):
    items = stem_slab.shape[3] // rows
    low = max(1, items * 3 // 8)
    high = items - low
    sent_low = batch_first(stem_slab, rows, 0, low)
    sent_low, factors = lax.optimization_barrier((sent_low, factors))
    stem_low = exchange(sent_low)
    held = scatter_branches(build_branch(factors[0]), branch_owner, rows, cols)
    cosine, sine = jnp.cos(entangle_phase), jnp.sin(entangle_phase)
    far = broadcast_orders(rows, cols)[2]
    for bit in far[:-1]:
        held = held + swap(held, "row", rows, bit)
    sent_high = batch_first(stem_slab, rows, low, high)
    held, sent_high, cosine, sine = lax.optimization_barrier((held, sent_high, cosine, sine))
    for bit in far[-1:]:
        held = held + swap(held, "row", rows, bit)
    stem_high = exchange(sent_high)
    branches = gather_branches(held, rows, cols)
    back_low = exchange(absorb(stem_low, branches, cosine, sine, weight=WEIGHT))
    some = min(2, high - 1)
    pairs, pieces = send_chips(absorb(stem_high, branches, cosine, sine, high - some, some))
    back_high = exchange(absorb(stem_high, branches, cosine, sine, 0, high - some))
    order = list(pieces)
    back_low, *came = lax.optimization_barrier((back_low, *[pieces[bit] for bit in order]))
    back_some = collect_chips(pairs, dict(zip(order, came)))
    return batch_last(rows_first(back_low, LAST), back_high, back_some)


def solution(mesh):
    return jax.shard_map(
        partial(on_device, rows=mesh.shape["row"], cols=mesh.shape["col"]),
        mesh=mesh,
        in_specs=(P(None, "row", None, "col"), P(("row", "col"), None, None, None, None), P(), P()),
        out_specs=P(None, "row", None, "col"),
        check_vma=False,
    )
```

```python
from functools import partial

import jax
import jax.numpy as jnp
from jax import lax
from jax.experimental import pallas as pl
from jax.experimental.pallas import tpu as pltpu
from jax.sharding import PartitionSpec as P

STEPS = 4
MIB = 1024 * 1024
WEIGHT = 1.8
LAST = 48
PER = (1, 2, 3)
DOT = partial(jnp.dot, precision=lax.Precision.HIGHEST)


def build_branch(owned):
    left_real, left_imag = (owned[0, 0], owned[0, 1])
    right_real, right_imag = (owned[1, 0], owned[1, 1])
    return jnp.stack(
        [
            DOT(left_real, right_real) - DOT(left_imag, right_imag),
            DOT(left_real, right_imag) + DOT(left_imag, right_real),
        ]
    )


def swap(array, axis, size, bit):
    return lax.ppermute(array, axis, [(i, i ^ bit) for i in range(size)])


def bits_of(size):
    return [1 << i for i in range(size.bit_length() - 1)]


def halve(held, stage):
    axis, size, index, bit = stage
    half = held.shape[0] // 2
    high = (index & bit) // bit
    keep = lax.dynamic_slice_in_dim(held, high * half, half, 0)
    send = lax.dynamic_slice_in_dim(held, (1 - high) * half, half, 0)
    return keep + swap(send, axis, size, bit)


def double(held, stage):
    axis, size, index, bit = stage
    other = swap(held, axis, size, bit)
    high = (index & bit) != 0
    return jnp.concatenate([jnp.where(high, other, held), jnp.where(high, held, other)], 0)


def broadcast_orders(rows, cols):
    row, col = lax.axis_index("row"), lax.axis_index("col")
    row_bits = bits_of(rows)
    first = [("row", rows, row, b) for b in row_bits[:1]]
    along_col = [("col", cols, col, b) for b in bits_of(cols)]
    along_row = [("row", rows, row, b) for b in row_bits[1:2]]
    return first, (along_col + along_row, along_row + along_col), row_bits[2:]


def scatter_branches(own, owners, rows, cols):
    first, orders, _ = broadcast_orders(rows, cols)
    me = lax.axis_index("row") * cols + lax.axis_index("col")
    mine = (owners == me).reshape(STEPS, 1, 1, 1)
    held = jnp.where(mine, own[None], 0.0).reshape(-1, own.shape[-1])
    for stage in first:
        held = halve(held, stage)
    halves = list(jnp.split(held, 2))
    for at in range(len(orders[0])):
        halves = [halve(part, order[at]) for part, order in zip(halves, orders)]
    return jnp.concatenate(halves, 0)


def gather_branches(held, rows, cols):
    first, orders, _ = broadcast_orders(rows, cols)
    halves = list(jnp.split(held, 2))
    for at in reversed(range(len(orders[0]))):
        halves = [double(part, order[at]) for part, order in zip(halves, orders)]
    held = jnp.concatenate(halves, 0)
    ((axis, size, _, bit),) = first
    width = held.shape[-1]
    shape = (STEPS // 2, 2, width, width)
    return held.reshape(shape), swap(held, axis, size, bit).reshape(shape)


def split(value):
    high = value.astype(jnp.bfloat16)
    low = (value - high.astype(jnp.float32)).astype(jnp.bfloat16)
    return high, low


def stack_branches(core, mine_ref, other_ref, even_ref, odd_ref):
    pair = STEPS // 2
    for step in range(STEPS):
        here = core == step // pair
        real, imag = (jnp.where(here, mine_ref[step % pair, i], other_ref[step % pair, i]) for i in range(2))
        if step % 2:
            real, imag = real.T, imag.T
        axis = 1 if step % 2 else 0
        (rh, rl), (ih, il) = split(real), split(imag)
        to_real = jnp.concatenate([rh, rh, rl, -ih, -ih, -il], axis)
        to_imag = jnp.concatenate([ih, ih, il, rh, rh, rl], axis)
        out = jnp.concatenate([to_real, to_imag], 1 - axis)
        if step % 2:
            odd_ref[step // 2] = out
        else:
            even_ref[step // 2] = out


def absorb_kernel(core_ref, stem_ref, mine_ref, other_ref, cos_ref, sin_ref, out_ref, even_ref, odd_ref):
    width = cos_ref.shape[1]
    items = range(stem_ref.shape[1])

    @pl.when(pl.program_id(0) == 0)
    def _():
        stack_branches(core_ref[0], mine_ref, other_ref, even_ref, odd_ref)

    held = [[stem_ref[:, item, i].reshape(width, width) for i in range(2)] for item in items]
    for step in range(STEPS):
        cosine, sine = cos_ref[step], sin_ref[step]
        for item in items:
            (rh, rl), (ih, il) = split(held[item][0]), split(held[item][1])
            if step % 2 == 0:
                stacked = jnp.concatenate([rh, rl, rh, ih, il, ih], 1)
                both = jnp.dot(stacked, even_ref[step // 2], preferred_element_type=jnp.float32)
                real, imag = both[:, :width], both[:, width:]
            else:
                stacked = jnp.concatenate([rh, rl, rh, ih, il, ih], 0)
                both = jnp.dot(odd_ref[step // 2], stacked, preferred_element_type=jnp.float32)
                real, imag = both[:width], both[width:]
            held[item] = [real * cosine - imag * sine, real * sine + imag * cosine]
    shape = (stem_ref.shape[0], stem_ref.shape[3], width)
    for item in items:
        for i in range(2):
            out_ref[:, item, i] = held[item][i].reshape(shape)


def in_hbm(*arrays):
    return [pltpu.with_memory_space_constraint(array, pltpu.HBM) for array in arrays]


def whole(array):
    return pl.BlockSpec(array.shape, lambda i: (0,) * array.ndim, pipeline_mode=pl.Buffered(1))


def absorb(stem, branches, cosine, sine, start=0, count=None, weight=1):
    peers, items, _, block, width = stem.shape
    count = items if count is None else count
    per = max(n for n in PER if count % n == 0 and start % n == 0)
    shape = (peers, per, 2, block, width)
    in_spec = pl.BlockSpec(shape, lambda i: (0, i + start // per, 0, 0, 0))
    out_spec = pl.BlockSpec(shape, lambda i: (0, i, 0, 0, 0))
    flops = count * STEPS * 12 * 2 * width**3
    core = (lax.axis_index("row") % 2).astype(jnp.int32).reshape(1)
    arrays = in_hbm(stem, *branches, cosine, sine)
    return pl.pallas_call(
        absorb_kernel,
        grid=(count // per,),
        in_specs=[pl.BlockSpec(memory_space=pltpu.SMEM), in_spec, *(whole(array) for array in arrays[1:])],
        out_specs=out_spec,
        out_shape=pltpu.HBM((peers, count, 2, block, width), jnp.float32),
        scratch_shapes=[
            pltpu.VMEM((STEPS // 2, 6 * width, 2 * width), jnp.bfloat16),
            pltpu.VMEM((STEPS // 2, 2 * width, 6 * width), jnp.bfloat16),
        ],
        cost_estimate=pl.CostEstimate(
            flops=int(flops * weight), bytes_accessed=8 * count * (stem.size // items), transcendentals=0
        ),
        compiler_params=pltpu.CompilerParams(vmem_limit_bytes=40 * MIB),
        name="absorb",
    )(core, *arrays)


def row_groups(parts, rows):
    return [(part, row) for part in range(parts) for row in range(0, rows, 8)]


def batch_first_kernel(start, stem_ref, out_ref, held, made, in_sem, out_sem):
    parts, rows = stem_ref.shape[:2]
    peers, items = out_ref.shape[:2]
    ins, outs = [], []
    for g, (part, row) in enumerate(row_groups(parts, rows)):
        ins.append(pltpu.make_async_copy(stem_ref.at[part, pl.ds(row, 8)], held.at[g], in_sem.at[g]))
        outs.append(
            [
                pltpu.make_async_copy(
                    made.at[g, pl.ds(item * peers, peers)],
                    out_ref.at[:, item, part, pl.ds(row, 8), :],
                    out_sem.at[g, item],
                )
                for item in range(items)
            ]
        )
    for copy in ins:
        copy.start()
    for g, copy in enumerate(ins):
        copy.wait()
        for i in range(8):
            made[g, :, i, :] = held[g, i][:, start : start + peers * items].T
        for out in outs[g]:
            out.start()
    for group in outs:
        for copy in group:
            copy.wait()


def batch_first(stem, peers, start, items):
    parts, rows, width, lanes = stem.shape
    groups = parts * rows // 8
    return pl.pallas_call(
        partial(batch_first_kernel, start * peers),
        in_specs=[pl.BlockSpec(memory_space=pl.ANY)],
        out_specs=pl.BlockSpec(memory_space=pl.ANY),
        out_shape=pltpu.HBM((peers, items, parts, rows, width), jnp.float32),
        scratch_shapes=[
            pltpu.VMEM((groups, 8, width, lanes), jnp.float32),
            pltpu.VMEM((groups, peers * items, 8, width), jnp.float32),
            pltpu.SemaphoreType.DMA((groups,)),
            pltpu.SemaphoreType.DMA((groups, items)),
        ],
        cost_estimate=pl.CostEstimate(flops=0, bytes_accessed=8 * stem.size, transcendentals=0),
        compiler_params=pltpu.CompilerParams(vmem_limit_bytes=24 * MIB),
        name="batch_first",
    )(*in_hbm(stem))


def rows_first_kernel(stem_ref, out_ref):
    peers, items = stem_ref.shape[:2]
    for i in range(out_ref.shape[1]):
        for item in range(items):
            out_ref[0, i, item * peers : (item + 1) * peers] = stem_ref[:, item, 0, i, :]


def rows_first(stem, weight):
    peers, items, parts, rows, width = stem.shape
    return pl.pallas_call(
        rows_first_kernel,
        grid=(parts, rows // 8),
        in_specs=[pl.BlockSpec((peers, items, 1, 8, width), lambda p, r: (0, 0, p, r, 0))],
        out_specs=pl.BlockSpec((1, 8, peers * items, width), lambda p, r: (p, r, 0, 0)),
        out_shape=pltpu.HBM((parts, rows, peers * items, width), jnp.float32),
        cost_estimate=pl.CostEstimate(flops=int(1e9 * weight), bytes_accessed=8 * stem.size, transcendentals=0),
        compiler_params=pltpu.CompilerParams(vmem_limit_bytes=24 * MIB),
        name="rows_first",
    )(*in_hbm(stem))


def batch_last_kernel(low_ref, *refs):
    *others, out_ref, low, made, low_sem, out_sem = refs
    parts, rows = out_ref.shape[:2]
    ins, outs = [], []
    for g, (part, row) in enumerate(row_groups(parts, rows)):
        ins.append(pltpu.make_async_copy(low_ref.at[part, pl.ds(row, 8)], low.at[g], low_sem.at[g]))
        outs.append(pltpu.make_async_copy(made.at[g], out_ref.at[part, pl.ds(row, 8)], out_sem.at[g]))
    for copy in ins:
        copy.start()
    for g, (part, row) in enumerate(row_groups(parts, rows)):
        ins[g].wait()
        for i in range(8):
            found = [ref[:, item, part, row + i, :] for ref in others for item in range(ref.shape[1])]
            made[g, i] = jnp.concatenate([low[g, i], *found], 0).T
        outs[g].start()
    for copy in outs:
        copy.wait()


def batch_last(low, *others):
    parts, rows, batch, width = low.shape
    lanes = batch + sum(other.shape[0] * other.shape[1] for other in others)
    groups = parts * rows // 8
    return pl.pallas_call(
        batch_last_kernel,
        in_specs=[pl.BlockSpec(memory_space=pl.ANY)] + [pl.BlockSpec(memory_space=pltpu.VMEM)] * len(others),
        out_specs=pl.BlockSpec(memory_space=pl.ANY),
        out_shape=jax.ShapeDtypeStruct((parts, rows, width, lanes), jnp.float32),
        scratch_shapes=[
            pltpu.VMEM((groups, 8, batch, width), jnp.float32),
            pltpu.VMEM((groups, 8, width, lanes), jnp.float32),
            pltpu.SemaphoreType.DMA((groups,)),
            pltpu.SemaphoreType.DMA((groups,)),
        ],
        compiler_params=pltpu.CompilerParams(vmem_limit_bytes=24 * MIB),
        name="batch_last",
    )(*in_hbm(low), *others)


def exchange(parts):
    return lax.all_to_all(parts, "row", 0, 0, tiled=True)


def pair_cores(parts):
    rows = parts.shape[0]
    core = lax.axis_index("row") % 2
    chips = parts.reshape(rows // 2, 2, *parts.shape[1:])
    same = lax.dynamic_index_in_dim(chips, core, 1, keepdims=False)
    other = lax.dynamic_index_in_dim(chips, 1 - core, 1, keepdims=False)
    other = swap(other, "row", rows, 1)
    return jnp.stack([jnp.where(core == 0, same, other), jnp.where(core == 0, other, same)], 1)


def send_chips(parts):
    rows = parts.shape[0]
    chip = lax.axis_index("row") // 2
    pairs = pair_cores(parts)
    pieces = {}
    for bit in reversed(range(1, rows // 2)):
        pieces[bit] = swap(lax.dynamic_index_in_dim(pairs, chip ^ bit, 0), "row", rows, 2 * bit)
    return pairs, pieces


def collect_chips(pairs, pieces):
    chip = lax.axis_index("row") // 2
    for bit, piece in pieces.items():
        pairs = lax.dynamic_update_index_in_dim(pairs, piece, chip ^ bit, 0)
    return pairs.reshape(-1, *pairs.shape[2:])


def on_device(stem_slab, factors, branch_owner, entangle_phase, *, rows, cols):
    items = stem_slab.shape[3] // rows
    low = max(1, items // 2)
    high = items - low
    sent_low = batch_first(stem_slab, rows, 0, low)
    sent_low, factors = lax.optimization_barrier((sent_low, factors))
    stem_low = exchange(sent_low)
    held = scatter_branches(build_branch(factors[0]), branch_owner, rows, cols)
    cosine, sine = jnp.cos(entangle_phase), jnp.sin(entangle_phase)
    far = broadcast_orders(rows, cols)[2]
    for bit in far[:-1]:
        held = held + swap(held, "row", rows, bit)
    sent_high = batch_first(stem_slab, rows, low, high)
    held, sent_high, cosine, sine = lax.optimization_barrier((held, sent_high, cosine, sine))
    for bit in far[-1:]:
        held = held + swap(held, "row", rows, bit)
    stem_high = exchange(sent_high)
    branches = gather_branches(held, rows, cols)
    back_low = exchange(absorb(stem_low, branches, cosine, sine, weight=WEIGHT))
    some = min(2, high - 1)
    pairs, pieces = send_chips(absorb(stem_high, branches, cosine, sine, high - some, some))
    back_high = exchange(absorb(stem_high, branches, cosine, sine, 0, high - some))
    order = list(pieces)
    back_low, *came = lax.optimization_barrier((back_low, *[pieces[bit] for bit in order]))
    back_some = collect_chips(pairs, dict(zip(order, came)))
    return batch_last(rows_first(back_low, LAST), back_high, back_some)


def solution(mesh):
    return jax.shard_map(
        partial(on_device, rows=mesh.shape["row"], cols=mesh.shape["col"]),
        mesh=mesh,
        in_specs=(P(None, "row", None, "col"), P(("row", "col"), None, None, None, None), P(), P()),
        out_specs=P(None, "row", None, "col"),
        check_vma=False,
    )
```

```python
from functools import partial

import jax
import jax.numpy as jnp
from jax import lax
from jax.experimental import pallas as pl
from jax.experimental.pallas import tpu as pltpu
from jax.sharding import PartitionSpec as P

STEPS = 4
MIB = 1024 * 1024
WEIGHT = 1.8
LAST = 48
PER = (1, 2, 3)
DOT = partial(jnp.dot, precision=lax.Precision.HIGHEST)


def build_branch(owned):
    left_real, left_imag = (owned[0, 0], owned[0, 1])
    right_real, right_imag = (owned[1, 0], owned[1, 1])
    return jnp.stack(
        [
            DOT(left_real, right_real) - DOT(left_imag, right_imag),
            DOT(left_real, right_imag) + DOT(left_imag, right_real),
        ]
    )


def swap(array, axis, size, bit):
    return lax.ppermute(array, axis, [(i, i ^ bit) for i in range(size)])


def bits_of(size):
    return [1 << i for i in range(size.bit_length() - 1)]


def halve(held, stage):
    axis, size, index, bit = stage
    half = held.shape[0] // 2
    high = (index & bit) // bit
    keep = lax.dynamic_slice_in_dim(held, high * half, half, 0)
    send = lax.dynamic_slice_in_dim(held, (1 - high) * half, half, 0)
    return keep + swap(send, axis, size, bit)


def double(held, stage):
    axis, size, index, bit = stage
    other = swap(held, axis, size, bit)
    high = (index & bit) != 0
    return jnp.concatenate([jnp.where(high, other, held), jnp.where(high, held, other)], 0)


def broadcast_orders(rows, cols):
    row, col = lax.axis_index("row"), lax.axis_index("col")
    row_bits = bits_of(rows)
    first = [("row", rows, row, b) for b in row_bits[:1]]
    along_col = [("col", cols, col, b) for b in bits_of(cols)]
    along_row = [("row", rows, row, b) for b in row_bits[1:2]]
    return first, (along_col + along_row, along_row + along_col), row_bits[2:]


def scatter_branches(own, owners, rows, cols):
    first, orders, _ = broadcast_orders(rows, cols)
    me = lax.axis_index("row") * cols + lax.axis_index("col")
    mine = (owners == me).reshape(STEPS, 1, 1, 1)
    held = jnp.where(mine, own[None], 0.0).reshape(-1, own.shape[-1])
    for stage in first:
        held = halve(held, stage)
    halves = list(jnp.split(held, 2))
    for at in range(len(orders[0])):
        halves = [halve(part, order[at]) for part, order in zip(halves, orders)]
    return halves


def gather_branches(halves, rows, cols):
    first, orders, _ = broadcast_orders(rows, cols)
    for at in reversed(range(len(orders[0]))):
        halves = [double(part, order[at]) for part, order in zip(halves, orders)]
    held = jnp.concatenate(halves, 0)
    ((axis, size, _, bit),) = first
    width = held.shape[-1]
    shape = (STEPS // 2, 2, width, width)
    return held.reshape(shape), swap(held, axis, size, bit).reshape(shape)


def split(value):
    high = value.astype(jnp.bfloat16)
    low = (value - high.astype(jnp.float32)).astype(jnp.bfloat16)
    return high, low


def stack_branches(core, mine_ref, other_ref, even_ref, odd_ref):
    pair = STEPS // 2
    for step in range(STEPS):
        here = core == step // pair
        real, imag = (jnp.where(here, mine_ref[step % pair, i], other_ref[step % pair, i]) for i in range(2))
        if step % 2:
            real, imag = real.T, imag.T
        axis = 1 if step % 2 else 0
        (rh, rl), (ih, il) = split(real), split(imag)
        to_real = jnp.concatenate([rh, rh, rl, -ih, -ih, -il], axis)
        to_imag = jnp.concatenate([ih, ih, il, rh, rh, rl], axis)
        out = jnp.concatenate([to_real, to_imag], 1 - axis)
        if step % 2:
            odd_ref[step // 2] = out
        else:
            even_ref[step // 2] = out


def absorb_kernel(core_ref, stem_ref, mine_ref, other_ref, cos_ref, sin_ref, out_ref, even_ref, odd_ref):
    width = cos_ref.shape[1]
    items = range(stem_ref.shape[1])

    @pl.when(pl.program_id(0) == 0)
    def _():
        stack_branches(core_ref[0], mine_ref, other_ref, even_ref, odd_ref)

    held = [[stem_ref[:, item, i].reshape(width, width) for i in range(2)] for item in items]
    for step in range(STEPS):
        cosine, sine = cos_ref[step], sin_ref[step]
        for item in items:
            (rh, rl), (ih, il) = split(held[item][0]), split(held[item][1])
            if step % 2 == 0:
                stacked = jnp.concatenate([rh, rl, rh, ih, il, ih], 1)
                both = jnp.dot(stacked, even_ref[step // 2], preferred_element_type=jnp.float32)
                real, imag = both[:, :width], both[:, width:]
            else:
                stacked = jnp.concatenate([rh, rl, rh, ih, il, ih], 0)
                both = jnp.dot(odd_ref[step // 2], stacked, preferred_element_type=jnp.float32)
                real, imag = both[:width], both[width:]
            held[item] = [real * cosine - imag * sine, real * sine + imag * cosine]
    shape = (stem_ref.shape[0], stem_ref.shape[3], width)
    for item in items:
        for i in range(2):
            out_ref[:, item, i] = held[item][i].reshape(shape)


def in_hbm(*arrays):
    return [pltpu.with_memory_space_constraint(array, pltpu.HBM) for array in arrays]


def whole(array):
    return pl.BlockSpec(array.shape, lambda i: (0,) * array.ndim, pipeline_mode=pl.Buffered(1))


def absorb(stem, branches, cosine, sine, start=0, count=None, weight=1):
    peers, items, _, block, width = stem.shape
    count = items if count is None else count
    per = max(n for n in PER if count % n == 0 and start % n == 0)
    shape = (peers, per, 2, block, width)
    in_spec = pl.BlockSpec(shape, lambda i: (0, i + start // per, 0, 0, 0))
    out_spec = pl.BlockSpec(shape, lambda i: (0, i, 0, 0, 0))
    flops = count * STEPS * 12 * 2 * width**3
    core = (lax.axis_index("row") % 2).astype(jnp.int32).reshape(1)
    arrays = in_hbm(stem, *branches, cosine, sine)
    return pl.pallas_call(
        absorb_kernel,
        grid=(count // per,),
        in_specs=[pl.BlockSpec(memory_space=pltpu.SMEM), in_spec, *(whole(array) for array in arrays[1:])],
        out_specs=out_spec,
        out_shape=pltpu.HBM((peers, count, 2, block, width), jnp.float32),
        scratch_shapes=[
            pltpu.VMEM((STEPS // 2, 6 * width, 2 * width), jnp.bfloat16),
            pltpu.VMEM((STEPS // 2, 2 * width, 6 * width), jnp.bfloat16),
        ],
        cost_estimate=pl.CostEstimate(
            flops=int(flops * weight), bytes_accessed=8 * count * (stem.size // items), transcendentals=0
        ),
        compiler_params=pltpu.CompilerParams(vmem_limit_bytes=40 * MIB),
        name="absorb",
    )(core, *arrays)


def row_groups(parts, rows):
    return [(part, row) for part in range(parts) for row in range(0, rows, 8)]


def batch_first_kernel(start, stem_ref, out_ref, held, made, in_sem, out_sem):
    parts, rows = stem_ref.shape[:2]
    peers, items = out_ref.shape[:2]
    ins, outs = [], []
    for g, (part, row) in enumerate(row_groups(parts, rows)):
        ins.append(pltpu.make_async_copy(stem_ref.at[part, pl.ds(row, 8)], held.at[g], in_sem.at[g]))
        outs.append(
            [
                pltpu.make_async_copy(
                    made.at[g, pl.ds(item * peers, peers)],
                    out_ref.at[:, item, part, pl.ds(row, 8), :],
                    out_sem.at[g, item],
                )
                for item in range(items)
            ]
        )
    for copy in ins:
        copy.start()
    for g, copy in enumerate(ins):
        copy.wait()
        for i in range(8):
            made[g, :, i, :] = held[g, i][:, start : start + peers * items].T
        for out in outs[g]:
            out.start()
    for group in outs:
        for copy in group:
            copy.wait()


def batch_first(stem, peers, start, items):
    parts, rows, width, lanes = stem.shape
    groups = parts * rows // 8
    return pl.pallas_call(
        partial(batch_first_kernel, start * peers),
        in_specs=[pl.BlockSpec(memory_space=pl.ANY)],
        out_specs=pl.BlockSpec(memory_space=pl.ANY),
        out_shape=pltpu.HBM((peers, items, parts, rows, width), jnp.float32),
        scratch_shapes=[
            pltpu.VMEM((groups, 8, width, lanes), jnp.float32),
            pltpu.VMEM((groups, peers * items, 8, width), jnp.float32),
            pltpu.SemaphoreType.DMA((groups,)),
            pltpu.SemaphoreType.DMA((groups, items)),
        ],
        cost_estimate=pl.CostEstimate(flops=0, bytes_accessed=8 * stem.size, transcendentals=0),
        compiler_params=pltpu.CompilerParams(vmem_limit_bytes=24 * MIB),
        name="batch_first",
    )(*in_hbm(stem))


def rows_first_kernel(stem_ref, out_ref):
    peers, items = stem_ref.shape[:2]
    for i in range(out_ref.shape[1]):
        for item in range(items):
            out_ref[0, i, item * peers : (item + 1) * peers] = stem_ref[:, item, 0, i, :]


def rows_first(stem, weight):
    peers, items, parts, rows, width = stem.shape
    return pl.pallas_call(
        rows_first_kernel,
        grid=(parts, rows // 8),
        in_specs=[pl.BlockSpec((peers, items, 1, 8, width), lambda p, r: (0, 0, p, r, 0))],
        out_specs=pl.BlockSpec((1, 8, peers * items, width), lambda p, r: (p, r, 0, 0)),
        out_shape=pltpu.HBM((parts, rows, peers * items, width), jnp.float32),
        cost_estimate=pl.CostEstimate(flops=int(1e9 * weight), bytes_accessed=8 * stem.size, transcendentals=0),
        compiler_params=pltpu.CompilerParams(vmem_limit_bytes=24 * MIB),
        name="rows_first",
    )(*in_hbm(stem))


def batch_last_kernel(low_ref, *refs):
    *others, out_ref, low, made, low_sem, out_sem = refs
    parts, rows = out_ref.shape[:2]
    ins, outs = [], []
    for g, (part, row) in enumerate(row_groups(parts, rows)):
        ins.append(pltpu.make_async_copy(low_ref.at[part, pl.ds(row, 8)], low.at[g], low_sem.at[g]))
        outs.append(pltpu.make_async_copy(made.at[g], out_ref.at[part, pl.ds(row, 8)], out_sem.at[g]))
    for copy in ins:
        copy.start()
    for g, (part, row) in enumerate(row_groups(parts, rows)):
        ins[g].wait()
        for i in range(8):
            found = [ref[:, item, part, row + i, :] for ref in others for item in range(ref.shape[1])]
            made[g, i] = jnp.concatenate([low[g, i], *found], 0).T
        outs[g].start()
    for copy in outs:
        copy.wait()


def batch_last(low, *others):
    parts, rows, batch, width = low.shape
    lanes = batch + sum(other.shape[0] * other.shape[1] for other in others)
    groups = parts * rows // 8
    return pl.pallas_call(
        batch_last_kernel,
        in_specs=[pl.BlockSpec(memory_space=pl.ANY)] + [pl.BlockSpec(memory_space=pltpu.VMEM)] * len(others),
        out_specs=pl.BlockSpec(memory_space=pl.ANY),
        out_shape=jax.ShapeDtypeStruct((parts, rows, width, lanes), jnp.float32),
        scratch_shapes=[
            pltpu.VMEM((groups, 8, batch, width), jnp.float32),
            pltpu.VMEM((groups, 8, width, lanes), jnp.float32),
            pltpu.SemaphoreType.DMA((groups,)),
            pltpu.SemaphoreType.DMA((groups,)),
        ],
        compiler_params=pltpu.CompilerParams(vmem_limit_bytes=24 * MIB),
        name="batch_last",
    )(*in_hbm(low), *others)


def exchange(parts):
    return lax.all_to_all(parts, "row", 0, 0, tiled=True)


def pair_cores(parts):
    rows = parts.shape[0]
    core = lax.axis_index("row") % 2
    chips = parts.reshape(rows // 2, 2, *parts.shape[1:])
    same = lax.dynamic_index_in_dim(chips, core, 1, keepdims=False)
    other = lax.dynamic_index_in_dim(chips, 1 - core, 1, keepdims=False)
    other = swap(other, "row", rows, 1)
    return jnp.stack([jnp.where(core == 0, same, other), jnp.where(core == 0, other, same)], 1)


def send_chips(parts):
    rows = parts.shape[0]
    chip = lax.axis_index("row") // 2
    pairs = pair_cores(parts)
    pieces = {}
    for bit in reversed(range(1, rows // 2)):
        pieces[bit] = swap(lax.dynamic_index_in_dim(pairs, chip ^ bit, 0), "row", rows, 2 * bit)
    return pairs, pieces


def collect_chips(pairs, pieces):
    chip = lax.axis_index("row") // 2
    for bit, piece in pieces.items():
        pairs = lax.dynamic_update_index_in_dim(pairs, piece, chip ^ bit, 0)
    return pairs.reshape(-1, *pairs.shape[2:])


def on_device(stem_slab, factors, branch_owner, entangle_phase, *, rows, cols):
    items = stem_slab.shape[3] // rows
    low = max(1, items // 2)
    high = items - low
    sent_low = batch_first(stem_slab, rows, 0, low)
    sent_low, factors = lax.optimization_barrier((sent_low, factors))
    stem_low = exchange(sent_low)
    halves = scatter_branches(build_branch(factors[0]), branch_owner, rows, cols)
    cosine, sine = jnp.cos(entangle_phase), jnp.sin(entangle_phase)
    far = broadcast_orders(rows, cols)[2]
    for bit in far[:-1]:
        halves = [half + swap(half, "row", rows, bit) for half in halves]
    sent_high = batch_first(stem_slab, rows, low, high)
    held = jnp.concatenate(halves, 0)
    held, sent_high, cosine, sine = lax.optimization_barrier((held, sent_high, cosine, sine))
    for bit in far[-1:]:
        held = held + swap(held, "row", rows, bit)
    stem_high = exchange(sent_high)
    branches = gather_branches(jnp.split(held, 2), rows, cols)
    back_low = exchange(absorb(stem_low, branches, cosine, sine, weight=WEIGHT))
    some = min(2, high - 1)
    pairs, pieces = send_chips(absorb(stem_high, branches, cosine, sine, high - some, some))
    back_high = exchange(absorb(stem_high, branches, cosine, sine, 0, high - some))
    order = list(pieces)
    back_low, *came = lax.optimization_barrier((back_low, *[pieces[bit] for bit in order]))
    back_some = collect_chips(pairs, dict(zip(order, came)))
    return batch_last(rows_first(back_low, LAST), back_high, back_some)


def solution(mesh):
    return jax.shard_map(
        partial(on_device, rows=mesh.shape["row"], cols=mesh.shape["col"]),
        mesh=mesh,
        in_specs=(P(None, "row", None, "col"), P(("row", "col"), None, None, None, None), P(), P()),
        out_specs=P(None, "row", None, "col"),
        check_vma=False,
    )
```
